256 devices in a mesh: row: 16 (over z_lo, y, core), col: 16 (over x, z_hi).
Axes of the slice: x: 4, y: 4, z: 8 (z_hi: 4, z_lo: 2; z = z_hi * 2 + z_lo), core: 2. Of those that a mesh axis runs over, the one named last changes fastest.
Arguments:
- pair_state: bfloat16 [32, 512, 6144], P(None, 'row', 'col'), may hold values from -6 to 6
- row_embed: bfloat16 [512, 512], P('row', 'col'), may hold values from -6 to 6
- col_embed: bfloat16 [6144, 512], P('col', 'row'), may hold values from -6 to 6
- row_proj: bfloat16 [512, 32], replicated, may hold values from -0.25 to 0.25
- col_proj: bfloat16 [512, 32], replicated, may hold values from -0.25 to 0.25
- conv_one: bfloat16 [9, 32, 32], replicated, may hold values from -0.375 to 0.375
- conv_two: bfloat16 [9, 32, 32], replicated, may hold values from -0.375 to 0.375
- bias_one: float32 [32], replicated, may hold values from -3 to 3
- bias_two: float32 [32], replicated, may hold values from -3 to 3
- cotangent: bfloat16 [32, 512, 6144], P(None, 'row', 'col'), may hold values from -3 to 3
Outputs:
- pair_out: bfloat16 [32, 512, 6144], P(None, 'row', 'col')
- state_grad: bfloat16 [32, 512, 6144], P(None, 'row', 'col')
- grad_row: float32 [512, 512], P('row', 'col')
- grad_col: float32 [6144, 512], P('col', 'row')
The draws below stay inside these ranges and needn't reach their ends.
All inputs are finite; a program needn't handle non-finite values.
Results may differ from the reference program's by a relative error of at most 0.0095.
Values may be sent and summed in bfloat16 or wider, within the bound.
No kernel may reach another device: no remote copies, remote signals or barrier semaphores. Data moves between devices by JAX's collectives and lax.ppermute only.
A program may use at most 128 MiB of HBM per device.

```python
import math
import jax
import jax.numpy as jnp
from jax import lax

D = 512
C = 32
NR = 512
NC = 6144


def levels(stream_key, extent, pieces, low, top_value):
    level = 1.0
    for dim, parts in pieces:
        heights = jax.random.uniform(jax.random.fold_in(jax.random.fold_in(stream_key, 6), dim), (parts,), jnp.float32, low / len(pieces), top_value / len(pieces))
        level = level * jnp.repeat(jnp.exp(heights), extent[dim] // parts).reshape((-1,) + (1,) * (len(extent) - 1 - dim))
    return level


def gaussian(rng, dims, width, limit, pieces=(), kind=jnp.bfloat16):
    drawn = width * jax.random.normal(rng, dims, jnp.float32)
    if pieces:
        drawn = drawn * levels(rng, dims, pieces, -0.22, 0.18)
    return jnp.clip(drawn, -limit, limit).astype(kind)


def setup_inputs(seed: int = 0) -> dict:
    arg_keys = jax.random.split(jax.random.key(seed), 11)
    return {
        "pair_state": gaussian(arg_keys[0], (C, NR, NC), 1.0, 6.0, ((1, 16), (2, 16))),
        "row_embed": gaussian(arg_keys[1], (NR, D), 1.0, 6.0, ((0, 16), (1, 16))),
        "col_embed": gaussian(arg_keys[2], (NC, D), 1.0, 6.0, ((0, 16), (1, 16))),
        "row_proj": gaussian(arg_keys[3], (D, C), D ** -0.5, 0.25),
        "col_proj": gaussian(arg_keys[4], (D, C), D ** -0.5, 0.25),
        "conv_one": gaussian(arg_keys[5], (9, C, C), (9 * C) ** -0.5, 0.375),
        "conv_two": gaussian(arg_keys[6], (9, C, C), (9 * C) ** -0.5, 0.375),
        "bias_one": gaussian(arg_keys[7], (C,), 0.5, 3.0, (), jnp.float32),
        "bias_two": gaussian(arg_keys[8], (C,), 0.5, 3.0, (), jnp.float32),
        "cotangent": gaussian(arg_keys[9], (C, NR, NC), 0.5, 3.0, ((1, 16), (2, 16))),
    }


def weight_matrix(weights, flipped):
    channels = weights.shape[1]
    if flipped:
        return jnp.transpose(weights, (2, 0, 1)).reshape(channels, 9 * channels)
    return jnp.transpose(weights, (1, 0, 2)).reshape(channels, 9 * channels)


def stack_windows(padded, flipped, height, breadth):
    windows = []
    for row_tap in range(3):
        for col_tap in range(3):
            shift_row = 4 * (row_tap - 1)
            shift_col = 4 * (col_tap - 1)
            if flipped:
                shift_row = -shift_row
                shift_col = -shift_col
            windows.append(padded[:, 4 + shift_row:4 + shift_row + height, 4 + shift_col:4 + shift_col + breadth])
    stacked = jnp.concatenate(windows, axis=0)
    return stacked.reshape(stacked.shape[0], height * breadth)


def conv_full(field, weights, flipped):
    channels = field.shape[0]
    height = field.shape[1]
    breadth = field.shape[2]
    padded = jnp.pad(field, ((0, 0), (4, 4), (4, 4)))
    stripe = math.gcd(height, 16)
    stripes = height // stripe
    matrix = weight_matrix(weights.astype(jnp.float32), flipped)

    def one_stripe(stripe_index):
        start = (stripe_index * stripe).astype(jnp.int32)
        slab = lax.dynamic_slice_in_dim(padded, start, stripe + 8, 1).astype(jnp.float32)
        stacked = stack_windows(slab, flipped, stripe, breadth)
        product = jnp.dot(matrix, stacked, precision=lax.Precision.HIGHEST)
        return product.reshape(channels, stripe, breadth)

    result = lax.map(one_stripe, jnp.arange(stripes, dtype=jnp.int32))
    return jnp.transpose(result, (1, 0, 2, 3)).reshape(channels, height, breadth)


def silu_slope(values):
    sigma = jax.nn.sigmoid(values)
    return sigma * (1.0 + values * (1.0 - sigma))


def reference(pair_state, row_embed, col_embed, row_proj, col_proj, conv_one, conv_two, bias_one, bias_two, cotangent):
    row_weights = row_proj.astype(jnp.float32)
    col_weights = col_proj.astype(jnp.float32)
    row_feat = jnp.dot(row_embed.astype(jnp.float32), row_weights, precision=lax.Precision.HIGHEST)
    col_feat = jnp.dot(col_embed.astype(jnp.float32), col_weights, precision=lax.Precision.HIGHEST)
    pair = (pair_state.astype(jnp.float32) + row_feat.T[:, :, None] + col_feat.T[:, None, :]).astype(jnp.bfloat16)
    hidden = conv_full(pair, conv_one, False) + bias_one[:, None, None]
    active = jax.nn.silu(hidden).astype(jnp.bfloat16)
    pair_out = (pair.astype(jnp.float32) + conv_full(active, conv_two, False) + bias_two[:, None, None]).astype(jnp.bfloat16)
    d_active = conv_full(cotangent, conv_two, True)
    d_hidden = (d_active * silu_slope(hidden)).astype(jnp.bfloat16)
    d_pair = cotangent.astype(jnp.float32) + conv_full(d_hidden, conv_one, True)
    state_grad = d_pair.astype(jnp.bfloat16)
    d_row_feat = jnp.sum(d_pair, axis=2).T
    d_col_feat = jnp.sum(d_pair, axis=1).T
    grad_row = jnp.dot(d_row_feat, row_weights.T, precision=lax.Precision.HIGHEST)
    grad_col = jnp.dot(d_col_feat, col_weights.T, precision=lax.Precision.HIGHEST)
    return pair_out, state_grad, grad_row, grad_col
```

```python
import jax
import jax.numpy as jnp
from jax import lax
from jax.experimental import pallas as pl
from jax.experimental.pallas import tpu as pltpu
from jax.sharding import PartitionSpec as P

F32 = jnp.float32
BF16 = jnp.bfloat16
C = 32
H = 32
W = 384
L = 512
R = 8
T = 128
N = 16
TILES = W // T
VMEM_LIMIT = 56 * 1024 * 1024


def params():
    return pltpu.CompilerParams(vmem_limit_bytes=VMEM_LIMIT)


def cost(flops, nbytes):
    return pl.CostEstimate(flops=flops, bytes_accessed=nbytes, transcendentals=0)


def full(shape):
    return pl.BlockSpec(shape, lambda *_: (0,) * len(shape))


def lane_iota(rows, lanes):
    return lax.broadcasted_iota(jnp.int32, (rows, lanes), 1)


def dot_nt(a, b):
    return lax.dot_general(a, b, (((1,), (1,)), ((), ())), preferred_element_type=F32)


def identity(size):
    rows = lax.broadcasted_iota(jnp.int32, (size, size), 0)
    return (rows == lane_iota(size, size)).astype(BF16)


def pack_kernel(state, cot, col_embed, row_embed, field, first, last, payload, rows):
    for half, source in ((0, state), (1, cot)):
        for tile in range(TILES):
            lanes = slice(tile * T, (tile + 1) * T)
            rows[tile] = source[:, :, lanes].astype(F32).reshape(C * H, T)
        for h in range(H):
            for tile in range(TILES):
                block = rows[tile, pl.ds(h, C, stride=H), :]
                field[h, half * C : (half + 1) * C, tile * T : (tile + 1) * T] = block.astype(BF16)
    lane = lane_iota(2 * C, T)
    for group in range(2):
        begin = jnp.zeros((2 * C, T), F32)
        end = jnp.zeros((2 * C, T), F32)
        for slot in range(16):
            h = group * 16 + slot
            here = (lane >= slot * R) & (lane < slot * R + R)
            left = field[h, :, 0:T].astype(F32)
            right = field[h, :, W - T : W].astype(F32)
            begin = jnp.where(here, pltpu.roll(left, slot * R, 1) if slot else left, begin)
            turn = (slot * R + R) % T
            end = jnp.where(here, pltpu.roll(right, turn, 1) if turn else right, end)
        first[:, group * T : (group + 1) * T] = begin.astype(BF16)
        last[:, group * T : (group + 1) * T] = end.astype(BF16)
    eye = identity(C)
    columns = dot_nt(eye, col_embed[...]).astype(BF16)
    edges = jnp.concatenate(
        [row_embed[0:R, :].astype(F32), row_embed[H - R : H, :].astype(F32), jnp.zeros((T - 2 * R, C), F32)],
        axis=0,
    ).astype(BF16)
    tail = dot_nt(eye, edges).astype(BF16)
    for peer in range(N):
        payload[peer, :, 0:W] = columns
        payload[peer, :, W:L] = tail


def pack(state, cot, col_embed, row_embed):
    return pl.pallas_call(
        pack_kernel,
        out_shape=(
            jax.ShapeDtypeStruct((H, 2 * C, L), BF16),
            jax.ShapeDtypeStruct((2 * C, 2 * T), BF16),
            jax.ShapeDtypeStruct((2 * C, 2 * T), BF16),
            jax.ShapeDtypeStruct((N, C, L), BF16),
        ),
        scratch_shapes=[pltpu.VMEM((TILES, C * H, T), F32)],
        compiler_params=params(),
        cost_estimate=cost(10**6, 4 * 10**6),
        name="pack",
    )(state, cot, col_embed, row_embed)


def sides_kernel(from_right, from_left, field_in, field):
    lane = lane_iota(2 * C, T)
    for h in range(H):
        group, slot = divmod(h, 16)
        lanes = slice(group * T, (group + 1) * T)
        right = from_right[:, lanes].astype(F32)
        left = from_left[:, lanes].astype(F32)
        if slot:
            right = pltpu.roll(right, T - slot * R, 1)
        turn = (T - R - slot * R) % T
        if turn:
            left = pltpu.roll(left, turn, 1)
        both = jnp.where(lane < R, right, jnp.where(lane >= T - R, left, 0.0))
        field[h, :, :] = both.astype(BF16)


def sides(from_right, from_left, field):
    return pl.pallas_call(
        sides_kernel,
        grid=(1,),
        out_shape=jax.ShapeDtypeStruct(field.shape, BF16),
        in_specs=[full((2 * C, 2 * T)), full((2 * C, 2 * T)), pl.BlockSpec(memory_space=pl.ANY)],
        out_specs=pl.BlockSpec((H, 2 * C, T), lambda i: (0, 0, TILES)),
        input_output_aliases={2: 0},
        compiler_params=params(),
        cost_estimate=cost(10**6, 10**6),
        name="sides",
    )(from_right, from_left, field)


def features_kernel(gathered, row_embed, col_proj_t, feat, payload):
    me = lax.axis_index("row")
    columns = jnp.dot(col_proj_t[...], gathered[...].reshape(N * C, L), preferred_element_type=F32)
    feat[...] = columns
    own = jnp.concatenate([row_embed[...].astype(F32), jnp.zeros((T - H, C), F32)], axis=0).astype(BF16)
    out = dot_nt(identity(C), own)
    above = gathered[lax.rem(me + N - 1, N), :, W:L].astype(F32)
    below = gathered[lax.rem(me + 1, N), :, W:L].astype(F32)
    high = columns.astype(BF16).astype(F32)
    low = columns - high
    lane = lane_iota(C, T)

    def put(out, start, source, origin):
        turn = (start - origin) % T
        moved = pltpu.roll(source, turn, 1) if turn else source
        return jnp.where((lane >= start) & (lane < start + R), moved, out)

    out = put(out, 32, above, 8)
    out = put(out, 40, below, 0)
    out = put(out, 48, high[:, 0:T], 0)
    out = put(out, 56, high[:, W - T : W], T - R)
    out = put(out, 64, low[:, 0:T], 0)
    out = put(out, 72, low[:, W - T : W], T - R)
    out = out.astype(BF16)
    for peer in range(N):
        payload[peer] = out


def features(gathered, row_embed, col_proj_t):
    return pl.pallas_call(
        features_kernel,
        out_shape=(jax.ShapeDtypeStruct((C, L), F32), jax.ShapeDtypeStruct((N, C, T), BF16)),
        compiler_params=params(),
        cost_estimate=cost(2 * C * L * L, 10**6),
        name="features",
    )(gathered, row_embed, col_proj_t)


def conv_row(matrix, rows, index):
    stacked = jnp.concatenate([rows[index], rows[index + 4], rows[index + 8]], axis=0)
    product = jnp.dot(matrix, stacked, preferred_element_type=F32)
    return product[C : 2 * C] + pltpu.roll(product[0:C], 4, 1) + pltpu.roll(product[2 * C : 3 * C], L - 4, 1)


def clear_outside(rows, count, depth):
    row = lax.axis_index("row")
    col = lax.axis_index("col")

    @pl.when(row == 0)
    def _():
        rows[0:depth] = jnp.zeros((depth, C, L), BF16)

    @pl.when(row == N - 1)
    def _():
        rows[count - depth : count] = jnp.zeros((depth, C, L), BF16)

    lane = lane_iota(C, T)

    @pl.when(col == 0)
    def _():
        for i in range(count):
            tile = rows[i, :, W:L].astype(F32)
            rows[i, :, W:L] = jnp.where(lane < T // 2, tile, 0.0).astype(BF16)

    @pl.when(col == N - 1)
    def _():
        for i in range(count):
            tile = rows[i, :, W:L].astype(F32)
            rows[i, :, W:L] = jnp.where(lane >= T // 2, tile, 0.0).astype(BF16)


def cot_kernel(field, above, below, matrix, out, rows):
    rows[0:R] = above[...]
    rows[R : R + H] = field[...]
    rows[R + H :] = below[...]
    clear_outside(rows, H + 2 * R, R)
    weights = matrix[...]

    @pl.loop(0, H + R, unroll=4)
    def _(i):
        out[i] = conv_row(weights, rows, i)


def half(rows, which):
    return pl.BlockSpec((rows, C, L), lambda i: (0, which, 0))


def cot_conv(field, above, below, matrix):
    return pl.pallas_call(
        cot_kernel,
        grid=(1,),
        out_shape=jax.ShapeDtypeStruct((H + R, C, L), F32),
        in_specs=[half(H, 1), half(R, 1), half(R, 1), full((3 * C, 3 * C))],
        out_specs=full((H + R, C, L)),
        scratch_shapes=[pltpu.VMEM((H + 2 * R, C, L), BF16)],
        compiler_params=params(),
        cost_estimate=cost(2 * 9 * C * C * L * (H + R), 4 * 10**6),
        name="cot_conv",
    )(field, above, below, matrix)


def store_row(scratch, h, value):
    for tile in range(TILES):
        scratch[tile, pl.ds(h, C, stride=H), :] = value[:, tile * T : (tile + 1) * T]


def write_map(out, scratch):
    for tile in range(TILES):
        out[:, :, tile * T : (tile + 1) * T] = scratch[tile].reshape(C, H, T).astype(BF16)


def main_kernel(
    field, above, below, cot, d_active, col_feat, gathered, row_proj_t, w_one, w_one_t, bias,
    active, pair, state_grad, col_part, row_part,
    rows, grads, scratch, col_sum,
):
    col = lax.axis_index("col")
    lane = lane_iota(C, T)
    row_feat = jnp.dot(row_proj_t[...], gathered[...].reshape(N * C, T), preferred_element_type=F32)
    right = gathered[lax.rem(col + 1, N)].astype(F32)
    left = gathered[lax.rem(col + N - 1, N)].astype(F32)
    right = pltpu.roll(right, T - 48, 1) + pltpu.roll(right, T - 64, 1)
    left = pltpu.roll(left, T - R - 56, 1) + pltpu.roll(left, T - R - 72, 1)
    side = jnp.where(lane < T // 2, right, left)
    columns = jnp.concatenate([col_feat[:, 0:W], side], axis=1)
    for i in range(H + 2 * R):
        if i < R:
            source, place = above[i], H + i
        elif i < R + H:
            source, place = field[i - R], i - R
        else:
            source, place = below[i - R - H], i
        value = source.astype(F32) + (columns + row_feat[:, place : place + 1])
        rows[i] = value.astype(BF16)
    clear_outside(rows, H + 2 * R, R)
    pair[...] = rows[R : R + H, :, 0:W]

    weights = w_one[...]
    first_bias = bias[...]

    @pl.loop(0, H + R, unroll=4)
    def _(i):
        hidden = conv_row(weights, rows, i) + first_bias
        sigma = 0.5 + 0.5 * jnp.tanh(0.5 * hidden)
        active[i] = (hidden * sigma).astype(BF16)
        slope = sigma * (1.0 + hidden * (1.0 - sigma))
        grads[i] = (d_active[i] * slope).astype(BF16)

    clear_outside(active, H + R, R // 2)
    clear_outside(grads, H + R, R // 2)
    weights_t = w_one_t[...]
    col_sum[...] = jnp.zeros((C, W), F32)

    def back(i, row_sum):
        d_pair = cot[i, :, 0:W].astype(F32) + conv_row(weights_t, grads, i)[:, 0:W]
        store_row(scratch, i, d_pair)
        col_sum[...] += d_pair
        total = jnp.sum(d_pair, axis=1, keepdims=True)
        return jnp.where(lane == i, total, row_sum)

    row_sum = lax.fori_loop(0, H, back, jnp.zeros((C, T), F32), unroll=4)
    write_map(state_grad, scratch)
    high = row_sum.astype(BF16)
    low = row_sum - high.astype(F32)
    row_out = (high.astype(F32) + pltpu.roll(low, H, 1)).astype(BF16)
    for peer in range(N):
        col_part[peer] = col_sum[...]
        row_part[peer] = row_out


def main_step(field, above, below, d_active, col_feat, gathered, row_proj_t, w_one, w_one_t, bias):
    return pl.pallas_call(
        main_kernel,
        grid=(1,),
        out_shape=(
            jax.ShapeDtypeStruct((H + R, C, L), BF16),
            jax.ShapeDtypeStruct((H, C, W), BF16),
            jax.ShapeDtypeStruct((C, H, W), BF16),
            jax.ShapeDtypeStruct((N, C, W), F32),
            jax.ShapeDtypeStruct((N, C, T), BF16),
        ),
        in_specs=[
            half(H, 0), half(R, 0), half(R, 0), half(H, 1), full((H + R, C, L)), full((C, L)),
            full((N, C, T)), full((C, N * C)), full((3 * C, 3 * C)), full((3 * C, 3 * C)), full((C, 1)),
        ],
        out_specs=(
            full((H + R, C, L)), full((H, C, W)), full((C, H, W)), full((N, C, W)), full((N, C, T)),
        ),
        scratch_shapes=[
            pltpu.VMEM((H + 2 * R, C, L), BF16),
            pltpu.VMEM((H + R, C, L), BF16),
            pltpu.VMEM((TILES, C * H, T), F32),
            pltpu.VMEM((C, W), F32),
        ],
        compiler_params=params(),
        cost_estimate=cost(4 * 9 * C * C * L * (H + R), 10**7),
        name="main_step",
    )(field, above, below, field, d_active, col_feat, gathered, row_proj_t, w_one, w_one_t, bias)


def out_kernel(active, pair, matrix, bias, out, scratch):
    weights = matrix[...]
    second_bias = bias[...]

    @pl.loop(0, H, unroll=4)
    def _(i):
        branch = conv_row(weights, active, i)[:, 0:W]
        store_row(scratch, i, pair[i].astype(F32) + branch + second_bias)

    write_map(out, scratch)


def out_step(active, pair, matrix, bias):
    return pl.pallas_call(
        out_kernel,
        out_shape=jax.ShapeDtypeStruct((C, H, W), BF16),
        scratch_shapes=[pltpu.VMEM((TILES, C * H, T), F32)],
        compiler_params=params(),
        cost_estimate=cost(2 * 9 * C * C * L * H, 4 * 10**6),
        name="out_step",
    )(active, pair, matrix, bias)


def taps(weights):
    return jnp.transpose(weights.reshape(3, 3, C, C), (1, 2, 0, 3)).reshape(3 * C, 3 * C)


def taps_transposed(weights):
    return jnp.transpose(weights.reshape(3, 3, C, C)[::-1, ::-1], (1, 3, 0, 2)).reshape(3 * C, 3 * C)


def everyone(blocks, axis):
    return lax.all_to_all(blocks, axis, 0, 0, tiled=True)


def on_device(
    pair_state, row_embed, col_embed, row_proj, col_proj, conv_one, conv_two, bias_one, bias_two, cotangent
):
    forward = [(i, (i + 1) % N) for i in range(N)]
    backward = [(j, i) for i, j in forward]
    field, first, last, payload = pack(pair_state, cotangent, col_embed, row_embed)
    from_left = lax.ppermute(last, "col", forward)
    from_right = lax.ppermute(first, "col", backward)
    field = sides(from_right, from_left, field)
    above = lax.ppermute(field[H - R :], "row", forward)
    below = lax.ppermute(field[:R], "row", backward)
    gathered = everyone(payload, "row")
    col_feat, payload = features(gathered, row_embed, col_proj.T)
    gathered = everyone(payload, "col")
    d_active = cot_conv(field, above, below, taps_transposed(conv_two))
    active, pair, state_grad, col_part, row_part = main_step(
        field, above, below, d_active, col_feat, gathered, row_proj.T,
        taps(conv_one), taps_transposed(conv_one), bias_one[:, None],
    )
    pair_out = out_step(active, pair, taps(conv_two), bias_two[:, None])
    row_all = everyone(row_part, "col").astype(F32).sum(0)
    row_all = row_all[:, 0:H] + row_all[:, H : 2 * H]
    col_all = everyone(col_part, "row").sum(0)
    row_slice = lax.dynamic_slice_in_dim(row_proj, lax.axis_index("col") * C, C, 0).astype(F32)
    col_slice = lax.dynamic_slice_in_dim(col_proj, lax.axis_index("row") * C, C, 0).astype(F32)
    contract = (((0,), (1,)), ((), ()))
    grad_row = lax.dot_general(row_all, row_slice, contract, precision=lax.Precision.HIGHEST)
    grad_col = lax.dot_general(col_all, col_slice, contract, precision=lax.Precision.HIGHEST)
    return pair_out, state_grad, grad_row, grad_col


def solution(mesh):
    placed = (
        P(None, "row", "col"),
        P("row", "col"),
        P("col", "row"),
        P(),
        P(),
        P(),
        P(),
        P(),
        P(),
        P(None, "row", "col"),
    )
    return jax.shard_map(
        on_device,
        mesh=mesh,
        in_specs=placed,
        out_specs=(P(None, "row", "col"), P(None, "row", "col"), P("row", "col"), P("col", "row")),
        check_vma=False,
    )
```

```python
import jax
import jax.numpy as jnp
from jax import lax
from jax.experimental import pallas as pl
from jax.experimental.pallas import tpu as pltpu
from jax.sharding import PartitionSpec as P

F32 = jnp.float32
BF16 = jnp.bfloat16
C = 32
H = 32
W = 384
L = 512
R = 8
T = 128
N = 16
TILES = W // T
VMEM_LIMIT = 20 * 1024 * 1024


def lane_iota(rows, lanes):
    return lax.broadcasted_iota(jnp.int32, (rows, lanes), 1)


def struct(*shape, dtype=BF16):
    return jax.ShapeDtypeStruct(shape, dtype)


def call(body, name, outs, args, flops, nbytes, scratch=()):
    return pl.pallas_call(
        body,
        out_shape=outs,
        scratch_shapes=list(scratch),
        compiler_params=pltpu.CompilerParams(vmem_limit_bytes=VMEM_LIMIT),
        cost_estimate=pl.CostEstimate(flops=flops, bytes_accessed=nbytes, transcendentals=0),
        name=name,
    )(*args)


def dot_nt(a, b):
    return lax.dot_general(a, b, (((1,), (1,)), ((), ())), preferred_element_type=F32)


def identity(size):
    rows = lax.broadcasted_iota(jnp.int32, (size, size), 0)
    return (rows == lane_iota(size, size)).astype(BF16)


def dot_tn(a, b):
    return lax.dot_general(a, b, (((0,), (0,)), ((), ())), preferred_element_type=F32)


def split(value):
    first = value.astype(BF16)
    rest = value - first.astype(F32)
    second = rest.astype(BF16)
    third = (rest - second.astype(F32)).astype(BF16)
    return first, second, third


def embed_kernel(col_embed_t, row_embed, payload):
    edges = jnp.concatenate(
        [row_embed[0:R, :].astype(F32), row_embed[H - R : H, :].astype(F32), jnp.zeros((T - 2 * R, C), F32)],
        axis=0,
    ).astype(BF16)
    tail = dot_nt(identity(C), edges).astype(BF16)
    for peer in range(N):
        payload[peer, :, 0:W] = col_embed_t[...]
        payload[peer, :, W:L] = tail


def pack_kernel(state, cot, field, first, last):
    for half, source in ((0, state), (1, cot)):
        for tile in range(TILES):
            lanes = slice(tile * T, (tile + 1) * T)
            field[:, half * C : (half + 1) * C, lanes] = jnp.swapaxes(source[:, :, lanes], 0, 1)
    lane = lane_iota(2 * C, T)
    for group in range(2):
        begin = jnp.zeros((2 * C, T), F32)
        end = jnp.zeros((2 * C, T), F32)
        for slot in range(16):
            h = group * 16 + slot
            here = (lane >= slot * R) & (lane < slot * R + R)
            left = field[h, :, 0:T].astype(F32)
            right = field[h, :, W - T : W].astype(F32)
            begin = jnp.where(here, pltpu.roll(left, slot * R, 1) if slot else left, begin)
            turn = (slot * R + R) % T
            end = jnp.where(here, pltpu.roll(right, turn, 1) if turn else right, end)
        first[:, group * T : (group + 1) * T] = begin.astype(BF16)
        last[:, group * T : (group + 1) * T] = end.astype(BF16)


def sides_kernel(from_right, from_left, field, side, top, bottom):
    lane = lane_iota(2 * C, T)
    for h in range(H):
        group, slot = divmod(h, 16)
        lanes = slice(group * T, (group + 1) * T)
        right = from_right[:, lanes].astype(F32)
        left = from_left[:, lanes].astype(F32)
        if slot:
            right = pltpu.roll(right, T - slot * R, 1)
        turn = (T - R - slot * R) % T
        if turn:
            left = pltpu.roll(left, turn, 1)
        both = jnp.where(lane < R, right, jnp.where(lane >= T - R, left, 0.0)).astype(BF16)
        side[h] = both
        if h < R:
            top[h, :, W:L] = both
        if h >= H - R:
            bottom[h - H + R, :, W:L] = both
    top[:, :, 0:W] = field[0:R]
    bottom[:, :, 0:W] = field[H - R : H]


def features_kernel(gathered, row_embed, col_proj_t, feat, payload):
    me = lax.axis_index("row")
    columns = jnp.dot(col_proj_t[...], gathered[...].reshape(N * C, L), preferred_element_type=F32)
    feat[...] = columns
    own = jnp.concatenate([row_embed[...].astype(F32), jnp.zeros((T - H, C), F32)], axis=0).astype(BF16)
    out = dot_nt(identity(C), own)
    above = gathered[lax.rem(me + N - 1, N), :, W:L].astype(F32)
    below = gathered[lax.rem(me + 1, N), :, W:L].astype(F32)
    high = columns.astype(BF16).astype(F32)
    low = columns - high
    lane = lane_iota(C, T)

    def put(out, start, source, origin):
        turn = (start - origin) % T
        moved = pltpu.roll(source, turn, 1) if turn else source
        return jnp.where((lane >= start) & (lane < start + R), moved, out)

    out = put(out, 32, above, 8)
    out = put(out, 40, below, 0)
    out = put(out, 48, high[:, 0:T], 0)
    out = put(out, 56, high[:, W - T : W], T - R)
    out = put(out, 64, low[:, 0:T], 0)
    out = put(out, 72, low[:, W - T : W], T - R)
    out = out.astype(BF16)
    for peer in range(N):
        payload[peer] = out


def band_kernel(conv_one, conv_two, one, one_t, two, two_t):
    eye = identity(C)

    def fill(out, weights, transposed):
        for b in range(3):
            pieces = []
            for a in range(3):
                if transposed:
                    pieces.append(dot_nt(eye, weights[3 * (2 - a) + 2 - b]))
                else:
                    pieces.append(weights[3 * a + b].astype(F32))
            pieces.append(jnp.zeros((C, 2 * T - 3 * C), F32))
            block = jnp.concatenate(pieces, axis=1)
            for t in range(5):
                moved = pltpu.roll(block, t * C, 1) if t else block
                out[(3 * t + b) * C : (3 * t + b + 1) * C, :] = moved.astype(BF16)

    fill(one, conv_one, False)
    fill(one_t, conv_one, True)
    fill(two, conv_two, False)
    fill(two_t, conv_two, True)


def conv_rows(band, rows, count):
    per = 5 if count == H + R else 4
    matrix = band[0 : 3 * C * per, 0 : C * (per + 2)]
    for residue in range(4):
        for group in range(2):
            start = residue + 4 * per * group
            stacked = jnp.concatenate([rows[start + 4 * s] for s in range(per + 2)], axis=0)
            product = jnp.dot(matrix, stacked, preferred_element_type=F32)
            for t in range(per):
                before, here, after = (product[(3 * t + b) * C : (3 * t + b + 1) * C] for b in range(3))
                yield start + 4 * t, here + pltpu.roll(before, 4, 1) + pltpu.roll(after, L - 4, 1)


def clear_outside(rows, count, depth):
    row = lax.axis_index("row")
    col = lax.axis_index("col")

    @pl.when(row == 0)
    def _():
        rows[0:depth] = jnp.zeros((depth, C, L), BF16)

    @pl.when(row == N - 1)
    def _():
        rows[count - depth : count] = jnp.zeros((depth, C, L), BF16)

    lane = lane_iota(C, T)

    @pl.when(col == 0)
    def _():
        for i in range(count):
            tile = rows[i, :, W:L].astype(F32)
            rows[i, :, W:L] = jnp.where(lane < T // 2, tile, 0.0).astype(BF16)

    @pl.when(col == N - 1)
    def _():
        for i in range(count):
            tile = rows[i, :, W:L].astype(F32)
            rows[i, :, W:L] = jnp.where(lane >= T // 2, tile, 0.0).astype(BF16)


def cot_kernel(field, side, above, below, band, out, rows):
    rows[0:R] = above[:, C : 2 * C, :]
    rows[R : R + H, :, 0:W] = field[:, C : 2 * C, :]
    rows[R : R + H, :, W:L] = side[:, C : 2 * C, :]
    rows[R + H :] = below[:, C : 2 * C, :]
    clear_outside(rows, H + 2 * R, R)
    for i, value in conv_rows(band, rows, H + R):
        out[i] = value


def main_kernel(
    field, side, above, below, d_active, col_feat, gathered, row_proj_t, one, one_t, bias,
    rows, active, state_grad, col_part, row_part,
    grads,
):
    col = lax.axis_index("col")
    lane = lane_iota(C, T)
    row_feat = jnp.dot(row_proj_t[...], gathered[...].reshape(N * C, T), preferred_element_type=F32)
    right = gathered[lax.rem(col + 1, N)].astype(F32)
    left = gathered[lax.rem(col + N - 1, N)].astype(F32)
    right = pltpu.roll(right, T - 48, 1) + pltpu.roll(right, T - 64, 1)
    left = pltpu.roll(left, T - R - 56, 1) + pltpu.roll(left, T - R - 72, 1)
    inner = col_feat[:, 0:W]
    outer = jnp.where(lane < T // 2, right, left)
    for i in range(H + 2 * R):
        if i < R:
            main, last, place = above[i, 0:C, 0:W], above[i, 0:C, W:L], H + i
        elif i < R + H:
            main, last, place = field[i - R, 0:C, :], side[i - R, 0:C, :], i - R
        else:
            main, last, place = below[i - R - H, 0:C, 0:W], below[i - R - H, 0:C, W:L], i
        feat = row_feat[:, place : place + 1]
        rows[i, :, 0:W] = (main.astype(F32) + (inner + feat)).astype(BF16)
        rows[i, :, W:L] = (last.astype(F32) + (outer + feat)).astype(BF16)
    clear_outside(rows, H + 2 * R, R)

    first_bias = bias[...]
    for i, value in conv_rows(one, rows, H + R):
        hidden = value + first_bias
        sigma = 0.5 + 0.5 * jnp.tanh(0.5 * hidden)
        active[i] = (hidden * sigma).astype(BF16)
        slope = sigma * (1.0 + hidden * (1.0 - sigma))
        grads[i] = (d_active[i] * slope).astype(BF16)
    clear_outside(active, H + R, R // 2)
    clear_outside(grads, H + R, R // 2)

    row_sum = jnp.zeros((C, T), F32)
    col_sum = jnp.zeros((C, W), F32)
    for i, value in conv_rows(one_t, grads, H):
        d_pair = field[i, C : 2 * C, :].astype(F32) + value[:, 0:W]
        state_grad[i] = d_pair.astype(BF16)
        col_sum = col_sum + d_pair
        total = jnp.sum(d_pair, axis=1, keepdims=True)
        row_sum = jnp.where(lane == i, total, row_sum)
    high = row_sum.astype(BF16)
    low = row_sum - high.astype(F32)
    row_out = (high.astype(F32) + pltpu.roll(low, H, 1)).astype(BF16)
    for peer in range(N):
        col_part[peer] = col_sum
        row_part[peer] = row_out


def out_kernel(active, rows, grad_rows, band, bias, pair_out, state_grad, scratch):
    second_bias = bias[...]
    for i, value in conv_rows(band, active, H):
        pair = rows[R + i, :, 0:W].astype(F32)
        scratch[i] = (pair + value[:, 0:W] + second_bias).astype(BF16)
    for tile in range(TILES):
        lanes = slice(tile * T, (tile + 1) * T)
        state_grad[:, :, lanes] = jnp.swapaxes(grad_rows[:, :, lanes], 0, 1)
        pair_out[:, :, lanes] = jnp.swapaxes(scratch[:, :, lanes], 0, 1)


def proj_slice(proj_t, axis):
    turn = lax.rem(L - lax.axis_index(axis) * C, L)
    return pltpu.roll(proj_t[...].astype(F32), turn, 1)[:, 0:T].astype(BF16)[:, 0:C]


def grad_row_kernel(gathered, row_proj_t, out):
    total = jnp.sum(gathered[...].astype(F32), axis=0)
    total = total + pltpu.roll(total, T - H, 1)
    weights = proj_slice(row_proj_t, "col")
    result = sum(dot_tn(part, weights) for part in split(total))
    out[...] = result[0:H, :]


def grad_col_kernel(gathered, col_proj_t, out):
    total = jnp.sum(gathered[...], axis=0)
    weights = proj_slice(col_proj_t, "row")
    out[...] = sum(dot_tn(weights, part) for part in split(total))


def everyone(blocks, axis):
    return lax.all_to_all(blocks, axis, 0, 0, tiled=True)


def on_device(
    pair_state, row_embed, col_embed, row_proj, col_proj, conv_one, conv_two, bias_one, bias_two, cotangent
):
    forward = [(i, (i + 1) % N) for i in range(N)]
    backward = [(j, i) for i, j in forward]
    payload = call(embed_kernel, "embed", struct(N, C, L), (col_embed.T, row_embed), 10**5, 6 * 10**5)
    gathered = everyone(payload, "row")
    field, first, last = call(
        pack_kernel, "pack", (struct(H, 2 * C, W), struct(2 * C, 2 * T), struct(2 * C, 2 * T)),
        (pair_state, cotangent), 10**6, 4 * 10**6,
    )
    from_left = lax.ppermute(last, "col", forward)
    from_right = lax.ppermute(first, "col", backward)
    side, top, bottom = call(
        sides_kernel, "sides", (struct(H, 2 * C, T), struct(R, 2 * C, L), struct(R, 2 * C, L)),
        (from_right, from_left, field), 10**6, 2 * 10**6,
    )
    above = lax.ppermute(bottom, "row", forward)
    below = lax.ppermute(top, "row", backward)
    band = struct(15 * C, 2 * T)
    one, one_t, two, two_t = call(
        band_kernel, "band", (band, band, band, band), (conv_one, conv_two), 10**6, 10**6
    )
    col_feat, payload = call(
        features_kernel, "features", (struct(C, L, dtype=F32), struct(N, C, T)),
        (gathered, row_embed, col_proj.T), 2 * C * L * L, 10**6,
    )
    gathered = everyone(payload, "col")
    d_active = call(
        cot_kernel, "cot_conv", struct(H + R, C, L, dtype=F32),
        (field, side, above, below, two_t), 3 * 10**9, 5 * 10**6,
        [pltpu.VMEM((H + 2 * R, C, L), BF16)],
    )
    rows, active, grad_rows, col_part, row_part = call(
        main_kernel, "main_step",
        (
            struct(H + 2 * R, C, L), struct(H + R, C, L), struct(H, C, W),
            struct(N, C, W, dtype=F32), struct(N, C, T),
        ),
        (field, side, above, below, d_active, col_feat, gathered, row_proj.T, one, one_t, bias_one[:, None]),
        6 * 10**9, 10**7, [pltpu.VMEM((H + R, C, L), BF16)],
    )
    pair_out, state_grad = call(
        out_kernel, "out_step", (struct(C, H, W), struct(C, H, W)),
        (active, rows, grad_rows, two, bias_two[:, None]), 3 * 10**9, 5 * 10**6,
        [pltpu.VMEM((H, C, W), BF16)],
    )
    row_all = everyone(row_part, "col")
    col_all = everyone(col_part, "row")
    grad_row = call(grad_row_kernel, "grad_row", struct(H, C, dtype=F32), (row_all, row_proj.T), 10**6, 10**5)
    grad_col = call(grad_col_kernel, "grad_col", struct(C, W, dtype=F32), (col_all, col_proj.T), 10**6, 10**6)
    return pair_out, state_grad, grad_row, grad_col.T


def solution(mesh):
    placed = (
        P(None, "row", "col"),
        P("row", "col"),
        P("col", "row"),
        P(),
        P(),
        P(),
        P(),
        P(),
        P(),
        P(None, "row", "col"),
    )
    return jax.shard_map(
        on_device,
        mesh=mesh,
        in_specs=placed,
        out_specs=(P(None, "row", "col"), P(None, "row", "col"), P("row", "col"), P("col", "row")),
        check_vma=False,
    )
```

```python
import jax
import jax.numpy as jnp
from jax import lax
from jax.experimental import pallas as pl
from jax.experimental.pallas import tpu as pltpu
from jax.sharding import PartitionSpec as P

F32 = jnp.float32
BF16 = jnp.bfloat16
C = 32
H = 32
W = 384
L = 512
R = 8
T = 128
N = 16
TILES = W // T
VMEM_LIMIT = 20 * 1024 * 1024


def lane_iota(rows, lanes):
    return lax.broadcasted_iota(jnp.int32, (rows, lanes), 1)


def struct(*shape, dtype=BF16):
    return jax.ShapeDtypeStruct(shape, dtype)


VMEM = pl.BlockSpec(memory_space=pltpu.VMEM)
HBM = pl.BlockSpec(memory_space=pltpu.HBM)
ANY = pl.BlockSpec(memory_space=pl.ANY)


def in_hbm(outs, places):
    if not places:
        return outs
    if not isinstance(outs, tuple):
        return pltpu.HBM(outs.shape, outs.dtype)
    return tuple(pltpu.HBM(o.shape, o.dtype) if p is HBM else o for o, p in zip(outs, places))


def call(body, name, outs, args, flops, nbytes, scratch=(), ins=None, places=None):
    several = isinstance(outs, tuple)
    if ins:
        args = [
            pltpu.with_memory_space_constraint(arg, pltpu.HBM) if spec is HBM else arg
            for arg, spec in zip(args, ins)
        ]
    return pl.pallas_call(
        body,
        out_shape=in_hbm(outs, places),
        in_specs=ins or [VMEM] * len(args),
        out_specs=places or ((VMEM,) * len(outs) if several else VMEM),
        scratch_shapes=list(scratch),
        compiler_params=pltpu.CompilerParams(vmem_limit_bytes=VMEM_LIMIT),
        cost_estimate=pl.CostEstimate(flops=flops, bytes_accessed=nbytes, transcendentals=0),
        name=name,
    )(*args)


def begin(source, target, sem):
    copy = pltpu.make_async_copy(source, target, sem)
    copy.start()
    return copy


def dot_nt(a, b):
    return lax.dot_general(a, b, (((1,), (1,)), ((), ())), preferred_element_type=F32)


def identity(size):
    rows = lax.broadcasted_iota(jnp.int32, (size, size), 0)
    return (rows == lane_iota(size, size)).astype(BF16)


def dot_tn(a, b):
    return lax.dot_general(a, b, (((0,), (0,)), ((), ())), preferred_element_type=F32)


def split(value):
    first = value.astype(BF16)
    rest = value - first.astype(F32)
    second = rest.astype(BF16)
    third = (rest - second.astype(F32)).astype(BF16)
    return first, second, third


def embed_kernel(col_embed_in, row_embed_in, payload, col_embed_t, row_embed, sem):
    copies = [begin(col_embed_in, col_embed_t, sem.at[0]), begin(row_embed_in, row_embed, sem.at[1])]
    for copy in copies:
        copy.wait()
    edges = jnp.concatenate(
        [row_embed[0:R, :].astype(F32), row_embed[H - R : H, :].astype(F32), jnp.zeros((T - 2 * R, C), F32)],
        axis=0,
    ).astype(BF16)
    tail = dot_nt(identity(C), edges).astype(BF16)
    for peer in range(N):
        payload[peer, :, 0:W] = col_embed_t[...]
        payload[peer, :, W:L] = tail


def pack_kernel(state_in, cot_in, field, first, last, state, cot, sem):
    copies = [begin(state_in, state, sem.at[0]), begin(cot_in, cot, sem.at[1])]
    for half, source in ((0, state), (1, cot)):
        copies[half].wait()
        for tile in range(TILES):
            lanes = slice(tile * T, (tile + 1) * T)
            field[:, half * C : (half + 1) * C, lanes] = jnp.swapaxes(source[:, :, lanes], 0, 1)
    lane = lane_iota(2 * C, T)
    for group in range(2):
        head = jnp.zeros((2 * C, T), F32)
        tail = jnp.zeros((2 * C, T), F32)
        for slot in range(16):
            h = group * 16 + slot
            here = (lane >= slot * R) & (lane < slot * R + R)
            left = field[h, :, 0:T].astype(F32)
            right = field[h, :, W - T : W].astype(F32)
            head = jnp.where(here, pltpu.roll(left, slot * R, 1) if slot else left, head)
            turn = (slot * R + R) % T
            tail = jnp.where(here, pltpu.roll(right, turn, 1) if turn else right, tail)
        first[:, group * T : (group + 1) * T] = head.astype(BF16)
        last[:, group * T : (group + 1) * T] = tail.astype(BF16)


def sides_kernel(from_right, from_left, field, side, top, bottom):
    lane = lane_iota(2 * C, T)
    for h in range(H):
        group, slot = divmod(h, 16)
        lanes = slice(group * T, (group + 1) * T)
        right = from_right[:, lanes].astype(F32)
        left = from_left[:, lanes].astype(F32)
        if slot:
            right = pltpu.roll(right, T - slot * R, 1)
        turn = (T - R - slot * R) % T
        if turn:
            left = pltpu.roll(left, turn, 1)
        both = jnp.where(lane < R, right, jnp.where(lane >= T - R, left, 0.0)).astype(BF16)
        side[h] = both
        if h < R:
            top[h, :, W:L] = both
        if h >= H - R:
            bottom[h - H + R, :, W:L] = both
    top[:, :, 0:W] = field[0:R]
    bottom[:, :, 0:W] = field[H - R : H]


def features_kernel(gathered, row_embed, col_proj_t, feat, payload):
    me = lax.axis_index("row")
    columns = jnp.dot(col_proj_t[...], gathered[...].reshape(N * C, L), preferred_element_type=F32)
    feat[...] = columns
    own = jnp.concatenate([row_embed[...].astype(F32), jnp.zeros((T - H, C), F32)], axis=0).astype(BF16)
    out = dot_nt(identity(C), own)
    above = gathered[lax.rem(me + N - 1, N), :, W:L].astype(F32)
    below = gathered[lax.rem(me + 1, N), :, W:L].astype(F32)
    high = columns.astype(BF16).astype(F32)
    low = columns - high
    lane = lane_iota(C, T)

    def put(out, start, source, origin):
        turn = (start - origin) % T
        moved = pltpu.roll(source, turn, 1) if turn else source
        return jnp.where((lane >= start) & (lane < start + R), moved, out)

    out = put(out, 32, above, 8)
    out = put(out, 40, below, 0)
    out = put(out, 48, high[:, 0:T], 0)
    out = put(out, 56, high[:, W - T : W], T - R)
    out = put(out, 64, low[:, 0:T], 0)
    out = put(out, 72, low[:, W - T : W], T - R)
    out = out.astype(BF16)
    for peer in range(N):
        payload[peer] = out


def band_kernel(conv_one, conv_two, one_out, one_t_out, two_out, two_t_out, one, one_t, two, two_t, sem):
    eye = identity(C)

    def fill(out, weights, transposed):
        for b in range(3):
            pieces = []
            for a in range(3):
                if transposed:
                    pieces.append(dot_nt(eye, weights[3 * (2 - a) + 2 - b]))
                else:
                    pieces.append(weights[3 * a + b].astype(F32))
            pieces.append(jnp.zeros((C, 2 * T - 3 * C), F32))
            block = jnp.concatenate(pieces, axis=1)
            for t in range(5):
                moved = pltpu.roll(block, t * C, 1) if t else block
                out[(3 * t + b) * C : (3 * t + b + 1) * C, :] = moved.astype(BF16)

    copies = []
    for k, (scratch, out, weights, transposed) in enumerate((
        (two_t, two_t_out, conv_two, True), (one, one_out, conv_one, False),
        (one_t, one_t_out, conv_one, True), (two, two_out, conv_two, False),
    )):
        fill(scratch, weights, transposed)
        copies.append(begin(scratch, out, sem.at[k]))
    for copy in copies:
        copy.wait()


def conv_rows(band, rows, count):
    per = 5 if count == H + R else 4
    matrix = band[0 : 3 * C * per, 0 : C * (per + 2)]
    for residue in range(4):
        for group in range(2):
            start = residue + 4 * per * group
            stacked = jnp.concatenate([rows[start + 4 * s] for s in range(per + 2)], axis=0)
            product = jnp.dot(matrix, stacked, preferred_element_type=F32)
            for t in range(per):
                before, here, after = (product[(3 * t + b) * C : (3 * t + b + 1) * C] for b in range(3))
                yield residue, per * group + t, here + pltpu.roll(before, 4, 1) + pltpu.roll(after, L - 4, 1)


def clear_outside(rows, count, depth):
    row = lax.axis_index("row")
    col = lax.axis_index("col")

    @pl.when(row == 0)
    def _():
        rows[0:depth] = jnp.zeros((depth, C, L), BF16)

    @pl.when(row == N - 1)
    def _():
        rows[count - depth : count] = jnp.zeros((depth, C, L), BF16)

    lane = lane_iota(C, T)

    @pl.when(col == 0)
    def _():
        for i in range(count):
            tile = rows[i, :, W:L].astype(F32)
            rows[i, :, W:L] = jnp.where(lane < T // 2, tile, 0.0).astype(BF16)

    @pl.when(col == N - 1)
    def _():
        for i in range(count):
            tile = rows[i, :, W:L].astype(F32)
            rows[i, :, W:L] = jnp.where(lane >= T // 2, tile, 0.0).astype(BF16)


def cot_kernel(field, side, above, below, band, out, rows, result, sem):
    rows[R : R + H, :, 0:W] = field[:, C : 2 * C, :]
    rows[R : R + H, :, W:L] = side[:, C : 2 * C, :]
    rows[0:R] = above[:, C : 2 * C, :]
    rows[R + H :] = below[:, C : 2 * C, :]
    clear_outside(rows, H + 2 * R, R)
    copies = []
    for residue, place, value in conv_rows(band, rows, H + R):
        result[residue, place] = value
        if place == (H + R) // 4 - 1:
            copies.append(begin(result.at[residue], out.at[residue], sem.at[residue]))
    for copy in copies:
        copy.wait()


def main_kernel(
    field, side, above_in, below_in, d_active_in, col_feat, gathered, row_proj_t, one_in, one_t_in, bias,
    pair_out, active_out, grad_out, col_part, row_part,
    rows, active, grads, above, below, d_active, one, one_t, grad_rows, sem,
):
    edges = [begin(above_in, above, sem.at[0]), begin(below_in, below, sem.at[1])]
    band = begin(one_in, one, sem.at[2])
    band_t = begin(one_t_in, one_t, sem.at[3])
    slopes = [begin(d_active_in.at[q], d_active.at[q], sem.at[4 + q]) for q in range(4)]
    col = lax.axis_index("col")
    lane = lane_iota(C, T)
    row_feat = jnp.dot(row_proj_t[...], gathered[...].reshape(N * C, T), preferred_element_type=F32)
    right = gathered[lax.rem(col + 1, N)].astype(F32)
    left = gathered[lax.rem(col + N - 1, N)].astype(F32)
    right = pltpu.roll(right, T - 48, 1) + pltpu.roll(right, T - 64, 1)
    left = pltpu.roll(left, T - R - 56, 1) + pltpu.roll(left, T - R - 72, 1)
    inner = col_feat[:, 0:W]
    outer = jnp.where(lane < T // 2, right, left)

    def assemble(i, main, last, place):
        feat = row_feat[:, place : place + 1]
        rows[i, :, 0:W] = (main.astype(F32) + (inner + feat)).astype(BF16)
        rows[i, :, W:L] = (last.astype(F32) + (outer + feat)).astype(BF16)

    for i in range(H):
        assemble(R + i, field[i, 0:C, :], side[i, 0:C, :], i)
    for copy in edges:
        copy.wait()
    for i in range(R):
        assemble(i, above[i, 0:C, 0:W], above[i, 0:C, W:L], H + i)
        assemble(R + H + i, below[i, 0:C, 0:W], below[i, 0:C, W:L], H + R + i)
    clear_outside(rows, H + 2 * R, R)
    copies = [begin(rows.at[R : R + H], pair_out, sem.at[8])]

    first_bias = bias[...]
    band.wait()
    for residue, place, value in conv_rows(one, rows, H + R):
        if place == 0:
            slopes[residue].wait()
        hidden = value + first_bias
        sigma = 0.5 + 0.5 * jnp.tanh(0.5 * hidden)
        active[residue + 4 * place] = (hidden * sigma).astype(BF16)
        slope = sigma * (1.0 + hidden * (1.0 - sigma))
        grads[residue + 4 * place] = (d_active[residue, place] * slope).astype(BF16)
    clear_outside(active, H + R, R // 2)
    clear_outside(grads, H + R, R // 2)
    copies.append(begin(active, active_out, sem.at[9]))

    band_t.wait()
    row_sum = jnp.zeros((C, T), F32)
    col_sum = jnp.zeros((C, W), F32)
    for residue, place, value in conv_rows(one_t, grads, H):
        i = residue + 4 * place
        d_pair = field[i, C : 2 * C, :].astype(F32) + value[:, 0:W]
        grad_rows[residue, place] = d_pair.astype(BF16)
        if place == H // 4 - 1:
            copies.append(begin(grad_rows.at[residue], grad_out.at[residue], sem.at[10 + residue]))
        col_sum = col_sum + d_pair
        total = jnp.sum(d_pair, axis=1, keepdims=True)
        row_sum = jnp.where(lane == i, total, row_sum)
    high = row_sum.astype(BF16)
    low = row_sum - high.astype(F32)
    row_out = (high.astype(F32) + pltpu.roll(low, H, 1)).astype(BF16)
    for peer in range(N):
        col_part[peer] = col_sum
        row_part[peer] = row_out
    for copy in copies:
        copy.wait()


def out_kernel(active, pair, band, bias, pair_out, scratch):
    second_bias = bias[...]
    for residue, place, value in conv_rows(band, active, H):
        i = residue + 4 * place
        scratch[i] = (pair[i, :, 0:W].astype(F32) + value[:, 0:W] + second_bias).astype(BF16)
    for tile in range(TILES):
        lanes = slice(tile * T, (tile + 1) * T)
        pair_out[:, :, lanes] = jnp.swapaxes(scratch[:, :, lanes], 0, 1)


def grad_kernel(grad_rows, state_grad, scratch):
    for i in range(H):
        scratch[i] = grad_rows[i % 4, i // 4]
    for tile in range(TILES):
        lanes = slice(tile * T, (tile + 1) * T)
        state_grad[:, :, lanes] = jnp.swapaxes(scratch[:, :, lanes], 0, 1)


def proj_slice(proj_t, axis):
    turn = lax.rem(L - lax.axis_index(axis) * C, L)
    return pltpu.roll(proj_t[...].astype(F32), turn, 1)[:, 0:T].astype(BF16)[:, 0:C]


def grad_row_kernel(gathered, row_proj_t, out):
    total = jnp.sum(gathered[...].astype(F32), axis=0)
    total = total + pltpu.roll(total, T - H, 1)
    weights = proj_slice(row_proj_t, "col")
    result = sum(dot_tn(part, weights) for part in split(total))
    out[...] = result[0:H, :]


def grad_col_kernel(gathered, col_proj_t, out):
    total = jnp.sum(gathered[...], axis=0)
    weights = proj_slice(col_proj_t, "row")
    out[...] = sum(dot_tn(weights, part) for part in split(total))


def everyone(blocks, axis):
    return lax.all_to_all(blocks, axis, 0, 0, tiled=True)


def on_device(
    pair_state, row_embed, col_embed, row_proj, col_proj, conv_one, conv_two, bias_one, bias_two, cotangent
):
    forward = [(i, (i + 1) % N) for i in range(N)]
    backward = [(j, i) for i, j in forward]
    payload = call(
        embed_kernel, "embed", struct(N, C, L), (col_embed.T, row_embed), 10**5, 6 * 10**5,
        [pltpu.VMEM((C, W), BF16), pltpu.VMEM((H, C), BF16), pltpu.SemaphoreType.DMA((2,))], [HBM, HBM],
    )
    gathered = everyone(payload, "row")
    field, first, last = call(
        pack_kernel, "pack", (struct(H, 2 * C, W), struct(2 * C, 2 * T), struct(2 * C, 2 * T)),
        (pair_state, cotangent), 10**6, 4 * 10**6,
        [pltpu.VMEM((C, H, W), BF16), pltpu.VMEM((C, H, W), BF16), pltpu.SemaphoreType.DMA((2,))], [HBM, HBM],
    )
    from_left = lax.ppermute(last, "col", forward)
    from_right = lax.ppermute(first, "col", backward)
    side, top, bottom = call(
        sides_kernel, "sides", (struct(H, 2 * C, T), struct(R, 2 * C, L), struct(R, 2 * C, L)),
        (from_right, from_left, field), 10**6, 2 * 10**6,
    )
    above = lax.ppermute(bottom, "row", forward)
    below = lax.ppermute(top, "row", backward)
    band = struct(15 * C, 2 * T)
    one, one_t, two, two_t = call(
        band_kernel, "band", (band, band, band, band), (conv_one, conv_two), 10**6, 10**6,
        places=(HBM,) * 4,
        scratch=[pltpu.VMEM(band.shape, BF16)] * 4 + [pltpu.SemaphoreType.DMA((4,))],
    )
    col_feat, payload = call(
        features_kernel, "features", (struct(C, L, dtype=F32), struct(N, C, T)),
        (gathered, row_embed, col_proj.T), 2 * C * L * L, 10**6,
    )
    gathered = everyone(payload, "col")
    spread = (4, (H + R) // 4, C, L)
    d_active = call(
        cot_kernel, "cot_conv", struct(*spread, dtype=F32),
        (field, side, above, below, two_t), 3 * 10**9, 5 * 10**6,
        [pltpu.VMEM((H + 2 * R, C, L), BF16), pltpu.VMEM(spread, F32), pltpu.SemaphoreType.DMA((4,))],
        places=HBM,
    )
    pair, active, grad_rows, col_part, row_part = call(
        main_kernel, "main_step",
        (
            struct(H, C, L), struct(H + R, C, L), struct(4, H // 4, C, W),
            struct(N, C, W, dtype=F32), struct(N, C, T),
        ),
        (field, side, above, below, d_active, col_feat, gathered, row_proj.T, one, one_t, bias_one[:, None]),
        6 * 10**9, 10**7,
        [
            pltpu.VMEM((H + 2 * R, C, L), BF16), pltpu.VMEM((H + R, C, L), BF16),
            pltpu.VMEM((H + R, C, L), BF16), pltpu.VMEM((R, 2 * C, L), BF16), pltpu.VMEM((R, 2 * C, L), BF16),
            pltpu.VMEM(spread, F32), pltpu.VMEM(band.shape, BF16), pltpu.VMEM(band.shape, BF16),
            pltpu.VMEM((4, H // 4, C, W), BF16), pltpu.SemaphoreType.DMA((14,)),
        ],
        [VMEM, VMEM, ANY, ANY, HBM, VMEM, VMEM, VMEM, HBM, HBM, VMEM],
        (HBM, HBM, HBM, VMEM, VMEM),
    )
    row_all = everyone(row_part, "col")
    pair_out = call(
        out_kernel, "out_step", struct(C, H, W), (active, pair, two, bias_two[:, None]),
        3 * 10**9, 5 * 10**6, [pltpu.VMEM((H, C, W), BF16)],
    )
    col_part, pair_out = lax.optimization_barrier((col_part, pair_out))
    col_all = everyone(col_part, "row")
    state_grad = call(
        grad_kernel, "state_grad", struct(C, H, W), (grad_rows,), 10**6, 2 * 10**6, [pltpu.VMEM((H, C, W), BF16)],
    )
    grad_row = call(grad_row_kernel, "grad_row", struct(H, C, dtype=F32), (row_all, row_proj.T), 10**6, 10**5)
    grad_col = call(grad_col_kernel, "grad_col", struct(C, W, dtype=F32), (col_all, col_proj.T), 10**6, 10**6)
    return pair_out, state_grad, grad_row, grad_col.T


def solution(mesh):
    placed = (
        P(None, "row", "col"),
        P("row", "col"),
        P("col", "row"),
        P(),
        P(),
        P(),
        P(),
        P(),
        P(),
        P(None, "row", "col"),
    )
    return jax.shard_map(
        on_device,
        mesh=mesh,
        in_specs=placed,
        out_specs=(P(None, "row", "col"), P(None, "row", "col"), P("row", "col"), P("col", "row")),
        check_vma=False,
    )
```

```python
import jax
import jax.numpy as jnp
from jax import lax
from jax.experimental import pallas as pl
from jax.experimental.pallas import tpu as pltpu
from jax.sharding import PartitionSpec as P

F32 = jnp.float32
BF16 = jnp.bfloat16
C = 32
H = 32
W = 384
L = 512
R = 8
T = 128
N = 16
TILES = W // T
VMEM_LIMIT = 24 * 1024 * 1024


def lane_iota(rows, lanes):
    return lax.broadcasted_iota(jnp.int32, (rows, lanes), 1)


def struct(*shape, dtype=BF16):
    return jax.ShapeDtypeStruct(shape, dtype)


VMEM = pl.BlockSpec(memory_space=pltpu.VMEM)
HBM = pl.BlockSpec(memory_space=pltpu.HBM)
ANY = pl.BlockSpec(memory_space=pl.ANY)


def in_hbm(outs, places):
    if not places:
        return outs
    if not isinstance(outs, tuple):
        return pltpu.HBM(outs.shape, outs.dtype)
    return tuple(pltpu.HBM(o.shape, o.dtype) if p is HBM else o for o, p in zip(outs, places))


def call(body, name, outs, args, flops, nbytes, scratch=(), ins=None, places=None):
    several = isinstance(outs, tuple)
    if ins:
        args = [
            pltpu.with_memory_space_constraint(arg, pltpu.HBM) if spec is HBM else arg
            for arg, spec in zip(args, ins)
        ]
    return pl.pallas_call(
        body,
        out_shape=in_hbm(outs, places),
        in_specs=ins or [VMEM] * len(args),
        out_specs=places or ((VMEM,) * len(outs) if several else VMEM),
        scratch_shapes=list(scratch),
        compiler_params=pltpu.CompilerParams(vmem_limit_bytes=VMEM_LIMIT),
        cost_estimate=pl.CostEstimate(flops=flops, bytes_accessed=nbytes, transcendentals=0),
        name=name,
    )(*args)


def begin(source, target, sem):
    copy = pltpu.make_async_copy(source, target, sem)
    copy.start()
    return copy


def dot_nt(a, b):
    return lax.dot_general(a, b, (((1,), (1,)), ((), ())), preferred_element_type=F32)


def identity(size):
    rows = lax.broadcasted_iota(jnp.int32, (size, size), 0)
    return (rows == lane_iota(size, size)).astype(BF16)


def dot_tn(a, b):
    return lax.dot_general(a, b, (((0,), (0,)), ((), ())), preferred_element_type=F32)


def split(value):
    first = value.astype(BF16)
    rest = value - first.astype(F32)
    second = rest.astype(BF16)
    third = (rest - second.astype(F32)).astype(BF16)
    return first, second, third


def pack_kernel(
    state_in, cot_in, col_embed_in, row_embed_in, field, first, last, payload,
    state, cot, col_embed_t, row_embed, sem,
):
    small = [begin(col_embed_in, col_embed_t, sem.at[0]), begin(row_embed_in, row_embed, sem.at[1])]
    pieces = []
    for tile in (0, 2, 1):
        lanes = slice(tile * T, (tile + 1) * T)
        for half, origin, target in ((0, state_in, state), (1, cot_in, cot)):
            copy = begin(origin.at[:, :, lanes], target.at[:, :, lanes], sem.at[2 + 2 * tile + half])
            pieces.append((half, target, lanes, copy))
    for copy in small:
        copy.wait()
    wide = row_embed[...].astype(F32)
    edges = jnp.concatenate(
        [wide[0:R], wide[H - R : H], jnp.zeros((T - 2 * R, C), F32)], axis=0
    ).astype(BF16)
    extra = dot_nt(identity(C), edges).astype(BF16)
    for peer in range(N):
        payload[peer, :, 0:W] = col_embed_t[...]
        payload[peer, :, W:L] = extra
    for half, source, lanes, copy in pieces:
        copy.wait()
        field[:, half * C : (half + 1) * C, lanes] = jnp.swapaxes(source[:, :, lanes], 0, 1)
    lane = lane_iota(2 * C, T)
    for group in range(2):
        head = jnp.zeros((2 * C, T), BF16)
        tail = jnp.zeros((2 * C, T), BF16)
        for slot in range(16):
            h = group * 16 + slot
            here = (lane >= slot * R) & (lane < slot * R + R)
            left = field[h, :, 0:T]
            right = field[h, :, W - T : W]
            head = jnp.where(here, pltpu.roll(left, slot * R, 1) if slot else left, head)
            turn = (slot * R + R) % T
            tail = jnp.where(here, pltpu.roll(right, turn, 1) if turn else right, tail)
        first[:, group * T : (group + 1) * T] = head
        last[:, group * T : (group + 1) * T] = tail


def sides_kernel(from_right, from_left, field, side, top, bottom):
    lane = lane_iota(2 * C, T)
    zero = jnp.zeros((2 * C, T), BF16)
    for h in range(H):
        group, slot = divmod(h, 16)
        lanes = slice(group * T, (group + 1) * T)
        right = from_right[:, lanes]
        left = from_left[:, lanes]
        if slot:
            right = pltpu.roll(right, T - slot * R, 1)
        turn = (T - R - slot * R) % T
        if turn:
            left = pltpu.roll(left, turn, 1)
        both = jnp.where(lane < R, right, jnp.where(lane >= T - R, left, zero))
        side[h] = both
        if h < R:
            top[h, :, W:L] = both
        if h >= H - R:
            bottom[h - H + R, :, W:L] = both
    top[:, :, 0:W] = field[0:R]
    bottom[:, :, 0:W] = field[H - R : H]


def features_kernel(gathered, row_embed, col_proj_t, feat, payload):
    me = lax.axis_index("row")
    columns = jnp.dot(col_proj_t[...], gathered[...].reshape(N * C, L), preferred_element_type=F32)
    feat[...] = columns
    own = jnp.concatenate([row_embed[...].astype(F32), jnp.zeros((T - H, C), F32)], axis=0).astype(BF16)
    out = dot_nt(identity(C), own)
    above = gathered[lax.rem(me + N - 1, N), :, W:L].astype(F32)
    below = gathered[lax.rem(me + 1, N), :, W:L].astype(F32)
    high = columns.astype(BF16).astype(F32)
    low = columns - high
    lane = lane_iota(C, T)

    def put(out, start, source, origin):
        turn = (start - origin) % T
        moved = pltpu.roll(source, turn, 1) if turn else source
        return jnp.where((lane >= start) & (lane < start + R), moved, out)

    out = put(out, 32, above, 8)
    out = put(out, 40, below, 0)
    out = put(out, 48, high[:, 0:T], 0)
    out = put(out, 56, high[:, W - T : W], T - R)
    out = put(out, 64, low[:, 0:T], 0)
    out = put(out, 72, low[:, W - T : W], T - R)
    out = out.astype(BF16)
    for peer in range(N):
        payload[peer] = out


BAND = 3 * C
TAPS = 9 * C
SPAN = 6 * T


def band_kernel(conv_one, conv_two, one_out, one_t_out, two_out, two_t_out, one, one_t, two, two_t, sem):
    eye = identity(C)

    def fill(out, weights, transposed):
        if transposed:
            stacked = jnp.concatenate([weights[8 - tap].astype(F32) for tap in range(9)], axis=0).astype(BF16)
            block = dot_nt(eye, stacked)
        else:
            block = jnp.concatenate([weights[tap].astype(F32) for tap in range(9)], axis=1)
        block = jnp.concatenate([block, jnp.zeros((C, SPAN - TAPS), F32)], axis=1)
        for t in range(5):
            moved = pltpu.roll(block, t * BAND, 1) if t else block
            out[t * C : (t + 1) * C, :] = moved.astype(BF16)

    copies = []
    for k, (scratch, out, weights, transposed) in enumerate((
        (two_t, two_t_out, conv_two, True), (one, one_out, conv_one, False),
        (one_t, one_t_out, conv_one, True), (two, two_out, conv_two, False),
    )):
        fill(scratch, weights, transposed)
        copies.append(begin(scratch, out, sem.at[k]))
    for copy in copies:
        copy.wait()


def put(rows, i, value):
    rows[i, C : 2 * C] = value


def shift(rows, count):
    for i in range(count):
        value = rows[i, C : 2 * C]
        rows[i, 0:C] = pltpu.roll(value, 4, 1)
        rows[i, 2 * C : 3 * C] = pltpu.roll(value, L - 4, 1)


def conv_rows(band, rows, count):
    per = 5 if count == H + R else 4
    matrix = band[0 : C * per, 0 : BAND * (per + 2)]
    for residue in range(4):
        for group in range(2):
            start = residue + 4 * per * group
            stacked = jnp.concatenate([rows[start + 4 * s] for s in range(per + 2)], axis=0)
            product = jnp.dot(matrix, stacked, preferred_element_type=F32)
            for t in range(per):
                yield residue, per * group + t, product[t * C : (t + 1) * C]


def inside():
    row = lax.axis_index("row")
    col = lax.axis_index("col")
    left = jnp.where(col > 0, 1.0, 0.0)
    right = jnp.where(col < N - 1, 1.0, 0.0)
    lanes = jnp.where(lane_iota(C, T) < T // 2, right, left)
    return lanes, jnp.where(row > 0, 1.0, 0.0), jnp.where(row < N - 1, 1.0, 0.0)


def cot_kernel(field, side, above, below, band, out, rows, result, sem):
    lanes, up, down = inside()
    for i in range(H):
        last = (side[i, C : 2 * C, :].astype(F32) * lanes).astype(BF16)
        put(rows, R + i, jnp.concatenate([field[i, C : 2 * C, :], last], axis=1))
    wide = jnp.concatenate([jnp.ones((C, W), F32), lanes], axis=1)
    for i in range(R):
        put(rows, i, (above[i, C : 2 * C, :].astype(F32) * (wide * up)).astype(BF16))
        put(rows, R + H + i, (below[i, C : 2 * C, :].astype(F32) * (wide * down)).astype(BF16))
    shift(rows, H + 2 * R)
    copies = []
    for residue, place, value in conv_rows(band, rows, H + R):
        result[residue, place] = value
        if place == (H + R) // 4 - 1:
            copies.append(begin(result.at[residue], out.at[residue], sem.at[residue]))
    for copy in copies:
        copy.wait()


def main_kernel(
    field, side, above_in, below_in, d_active_in, col_feat, gathered, row_proj_t, one_in, one_t_in, bias,
    pair_out, active_out, grad_out, col_part, row_part,
    rows, active, grads, above, below, d_active, one, one_t, grad_rows, sums, sem,
):
    edges = [begin(above_in, above, sem.at[0]), begin(below_in, below, sem.at[1])]
    band = begin(one_in, one, sem.at[2])
    slopes = [begin(d_active_in.at[q], d_active.at[q], sem.at[4 + q]) for q in range(4)]
    band_t = begin(one_t_in, one_t, sem.at[3])
    col = lax.axis_index("col")
    lane = lane_iota(C, T)
    lanes, up, down = inside()
    row_feat = jnp.dot(row_proj_t[...], gathered[...].reshape(N * C, T), preferred_element_type=F32)
    right = gathered[lax.rem(col + 1, N)].astype(F32)
    left = gathered[lax.rem(col + N - 1, N)].astype(F32)
    right = pltpu.roll(right, T - 48, 1) + pltpu.roll(right, T - 64, 1)
    left = pltpu.roll(left, T - R - 56, 1) + pltpu.roll(left, T - R - 72, 1)
    columns = jnp.concatenate([col_feat[:, 0:W], jnp.where(lane < T // 2, right, left)], axis=1)
    wide = jnp.concatenate([jnp.ones((C, W), F32), lanes], axis=1)

    def assemble(value, place):
        return value.astype(F32) + (columns + row_feat[:, place : place + 1])

    for i in range(H):
        value = assemble(jnp.concatenate([field[i, 0:C, :], side[i, 0:C, :]], axis=1), i)
        value = jnp.concatenate([value[:, 0:W], value[:, W:L] * lanes], axis=1)
        put(rows, R + i, value.astype(BF16))
    for copy in edges:
        copy.wait()
    for i in range(R):
        put(rows, i, (assemble(above[i, 0:C, :], H + i) * (wide * up)).astype(BF16))
        place = R + H + i
        put(rows, place, (assemble(below[i, 0:C, :], place) * (wide * down)).astype(BF16))
    shift(rows, H + 2 * R)
    copies = [begin(rows.at[R : R + H, C : 2 * C, 0:W], pair_out, sem.at[8])]

    first_bias = bias[...]
    band.wait()
    for residue, place, value in conv_rows(one, rows, H + R):
        if place == 0:
            slopes[residue].wait()
        i = residue + 4 * place
        hidden = value + first_bias
        sigma = 0.5 + 0.5 * jnp.tanh(0.5 * hidden)
        slope = sigma * (1.0 + hidden * (1.0 - sigma))

        def clip(value):
            value = jnp.concatenate([value[:, 0:W], value[:, W:L] * lanes], axis=1)
            if i < R // 2:
                value = value * up
            if i >= H + R // 2:
                value = value * down
            return value.astype(BF16)

        active[i] = clip(hidden * sigma)
        put(grads, i, clip(d_active[residue, place] * slope))
    copies.append(begin(active, active_out, sem.at[9]))

    shift(grads, H + R)
    band_t.wait()
    col_sum = jnp.zeros((C, W), F32)
    for residue, place, value in conv_rows(one_t, grads, H):
        i = residue + 4 * place
        d_pair = field[i, C : 2 * C, :].astype(F32) + value[:, 0:W]
        grad_rows[residue, place] = d_pair.astype(BF16)
        if place == H // 4 - 1:
            copies.append(begin(grad_rows.at[residue], grad_out.at[residue], sem.at[10 + residue]))
        col_sum = col_sum + d_pair
        sums[i * C : (i + 1) * C, :] = d_pair[:, 0:T] + d_pair[:, T : 2 * T] + d_pair[:, 2 * T : W]
    col_out = col_sum.astype(BF16)
    for peer in range(N):
        col_part[peer] = col_out
    partial = sums[...]
    high = partial.astype(BF16)
    low = (partial - high.astype(F32)).astype(BF16)
    ones = jnp.ones((2 * T, T), BF16)
    totals = jnp.dot(jnp.concatenate([high, low], axis=1), ones, preferred_element_type=F32)
    row_sum = jnp.zeros((C, T), F32)
    for i in range(H):
        row_sum = jnp.where(lane == i, totals[i * C : (i + 1) * C], row_sum)
    high = row_sum.astype(BF16)
    low = row_sum - high.astype(F32)
    row_out = (high.astype(F32) + pltpu.roll(low, H, 1)).astype(BF16)
    for peer in range(N):
        row_part[peer] = row_out
    for copy in copies:
        copy.wait()


def out_kernel(active, pair, band, bias, pair_out, rows, scratch):
    second_bias = bias[...]
    for i in range(H + R):
        put(rows, i, active[i])
    shift(rows, H + R)
    for residue, place, value in conv_rows(band, rows, H):
        i = residue + 4 * place
        scratch[i] = (pair[i].astype(F32) + value[:, 0:W] + second_bias).astype(BF16)
    for tile in range(TILES):
        lanes = slice(tile * T, (tile + 1) * T)
        pair_out[:, :, lanes] = jnp.swapaxes(scratch[:, :, lanes], 0, 1)


def grad_kernel(grad_rows, state_grad, scratch):
    for i in range(H):
        scratch[i] = grad_rows[i % 4, i // 4]
    for tile in range(TILES):
        lanes = slice(tile * T, (tile + 1) * T)
        state_grad[:, :, lanes] = jnp.swapaxes(scratch[:, :, lanes], 0, 1)


def proj_slice(proj_t, axis):
    turn = lax.rem(L - lax.axis_index(axis) * C, L)
    return pltpu.roll(proj_t[...].astype(F32), turn, 1)[:, 0:T].astype(BF16)[:, 0:C]


def grad_row_kernel(gathered, row_proj_t, out):
    total = jnp.sum(gathered[...].astype(F32), axis=0)
    total = total + pltpu.roll(total, T - H, 1)
    weights = proj_slice(row_proj_t, "col")
    result = sum(dot_tn(part, weights) for part in split(total))
    out[...] = result[0:H, :]


def grad_col_kernel(gathered, col_proj_t, out):
    total = jnp.sum(gathered[...].astype(F32), axis=0)
    weights = proj_slice(col_proj_t, "row")
    out[...] = sum(dot_tn(weights, part) for part in split(total))


def everyone(blocks, axis):
    return lax.all_to_all(blocks, axis, 0, 0, tiled=True)


def on_device(
    pair_state, row_embed, col_embed, row_proj, col_proj, conv_one, conv_two, bias_one, bias_two, cotangent
):
    forward = [(i, (i + 1) % N) for i in range(N)]
    backward = [(j, i) for i, j in forward]
    field, first, last, payload = call(
        pack_kernel, "pack",
        (struct(H, 2 * C, W), struct(2 * C, 2 * T), struct(2 * C, 2 * T), struct(N, C, L)),
        (pair_state, cotangent, col_embed.T, row_embed), 10**6, 4 * 10**6,
        [
            pltpu.VMEM((C, H, W), BF16), pltpu.VMEM((C, H, W), BF16), pltpu.VMEM((C, W), BF16),
            pltpu.VMEM((H, C), BF16), pltpu.SemaphoreType.DMA((8,)),
        ],
        [HBM] * 4,
    )
    from_left = lax.ppermute(last, "col", forward)
    from_right = lax.ppermute(first, "col", backward)
    band = struct(C * 5, SPAN)
    one, one_t, two, two_t = call(
        band_kernel, "band", (band, band, band, band), (conv_one, conv_two), 10**6, 10**6,
        places=(HBM,) * 4,
        scratch=[pltpu.VMEM(band.shape, BF16)] * 4 + [pltpu.SemaphoreType.DMA((4,))],
    )
    from_left, from_right, one = lax.optimization_barrier((from_left, from_right, one))
    gathered = everyone(payload, "row")
    side, top, bottom = call(
        sides_kernel, "sides", (struct(H, 2 * C, T), struct(R, 2 * C, L), struct(R, 2 * C, L)),
        (from_right, from_left, field), 10**6, 2 * 10**6,
    )
    above = lax.ppermute(bottom, "row", forward)
    below = lax.ppermute(top, "row", backward)
    col_feat, payload = call(
        features_kernel, "features", (struct(C, L, dtype=F32), struct(N, C, T)),
        (gathered, row_embed, col_proj.T), 2 * C * L * L, 10**6,
    )
    gathered = everyone(payload, "col")
    spread = (4, (H + R) // 4, C, L)
    d_active = call(
        cot_kernel, "cot_conv", struct(*spread, dtype=F32),
        (field, side, above, below, two_t), 3 * 10**9, 5 * 10**6,
        [pltpu.VMEM((H + 2 * R, BAND, L), BF16), pltpu.VMEM(spread, F32), pltpu.SemaphoreType.DMA((4,))],
        places=HBM,
    )
    pair, active, grad_rows, col_part, row_part = call(
        main_kernel, "main_step",
        (
            struct(H, C, W), struct(H + R, C, L), struct(4, H // 4, C, W),
            struct(N, C, W), struct(N, C, T),
        ),
        (field, side, above, below, d_active, col_feat, gathered, row_proj.T, one, one_t, bias_one[:, None]),
        6 * 10**9, 10**7,
        [
            pltpu.VMEM((H + 2 * R, BAND, L), BF16), pltpu.VMEM((H + R, C, L), BF16),
            pltpu.VMEM((H + R, BAND, L), BF16), pltpu.VMEM((R, 2 * C, L), BF16), pltpu.VMEM((R, 2 * C, L), BF16),
            pltpu.VMEM(spread, F32), pltpu.VMEM(band.shape, BF16), pltpu.VMEM(band.shape, BF16),
            pltpu.VMEM((4, H // 4, C, W), BF16), pltpu.VMEM((H * C, T), F32), pltpu.SemaphoreType.DMA((14,)),
        ],
        [VMEM, VMEM, ANY, ANY, HBM, VMEM, VMEM, VMEM, HBM, HBM, VMEM],
        (HBM, HBM, HBM, VMEM, VMEM),
    )
    row_all = everyone(row_part, "col")
    pair_out = call(
        out_kernel, "out_step", struct(C, H, W), (active, pair, two, bias_two[:, None]),
        3 * 10**9, 5 * 10**6, [pltpu.VMEM((H + R, BAND, L), BF16), pltpu.VMEM((H, C, W), BF16)],
    )
    col_part, pair_out = lax.optimization_barrier((col_part, pair_out))
    col_all = everyone(col_part, "row")
    state_grad = call(
        grad_kernel, "state_grad", struct(C, H, W), (grad_rows,), 10**6, 2 * 10**6, [pltpu.VMEM((H, C, W), BF16)],
    )
    grad_row = call(grad_row_kernel, "grad_row", struct(H, C, dtype=F32), (row_all, row_proj.T), 10**6, 10**5)
    grad_col = call(grad_col_kernel, "grad_col", struct(C, W, dtype=F32), (col_all, col_proj.T), 10**6, 10**6)
    return pair_out, state_grad, grad_row, grad_col.T


def solution(mesh):
    placed = (
        P(None, "row", "col"),
        P("row", "col"),
        P("col", "row"),
        P(),
        P(),
        P(),
        P(),
        P(),
        P(),
        P(None, "row", "col"),
    )
    return jax.shard_map(
        on_device,
        mesh=mesh,
        in_specs=placed,
        out_specs=(P(None, "row", "col"), P(None, "row", "col"), P("row", "col"), P("col", "row")),
        check_vma=False,
    )
```

```python
import jax
import jax.numpy as jnp
from jax import lax
from jax.experimental import pallas as pl
from jax.experimental.pallas import tpu as pltpu
from jax.sharding import PartitionSpec as P

F32 = jnp.float32
BF16 = jnp.bfloat16
C = 32
H = 32
W = 384
L = 512
R = 8
T = 128
N = 16
TILES = W // T
VMEM_LIMIT = 30 * 1024 * 1024


def lane_iota(rows, lanes):
    return lax.broadcasted_iota(jnp.int32, (rows, lanes), 1)


def struct(*shape, dtype=BF16):
    return jax.ShapeDtypeStruct(shape, dtype)


VMEM = pl.BlockSpec(memory_space=pltpu.VMEM)
HBM = pl.BlockSpec(memory_space=pltpu.HBM)
ANY = pl.BlockSpec(memory_space=pl.ANY)


def in_hbm(outs, places):
    if not places:
        return outs
    if not isinstance(outs, tuple):
        return pltpu.HBM(outs.shape, outs.dtype)
    return tuple(pltpu.HBM(o.shape, o.dtype) if p is HBM else o for o, p in zip(outs, places))


def call(body, name, outs, args, flops, nbytes, scratch=(), ins=None, places=None):
    several = isinstance(outs, tuple)
    if ins:
        args = [
            pltpu.with_memory_space_constraint(arg, pltpu.HBM) if spec is HBM else arg
            for arg, spec in zip(args, ins)
        ]
    return pl.pallas_call(
        body,
        out_shape=in_hbm(outs, places),
        in_specs=ins or [VMEM] * len(args),
        out_specs=places or ((VMEM,) * len(outs) if several else VMEM),
        scratch_shapes=list(scratch),
        compiler_params=pltpu.CompilerParams(vmem_limit_bytes=VMEM_LIMIT),
        cost_estimate=pl.CostEstimate(flops=flops, bytes_accessed=nbytes, transcendentals=0),
        name=name,
    )(*args)


def begin(source, target, sem):
    copy = pltpu.make_async_copy(source, target, sem)
    copy.start()
    return copy


def dot_nt(a, b):
    return lax.dot_general(a, b, (((1,), (1,)), ((), ())), preferred_element_type=F32)


def identity(size):
    rows = lax.broadcasted_iota(jnp.int32, (size, size), 0)
    return (rows == lane_iota(size, size)).astype(BF16)


def dot_tn(a, b):
    return lax.dot_general(a, b, (((0,), (0,)), ((), ())), preferred_element_type=F32)


def split(value):
    first = value.astype(BF16)
    rest = value - first.astype(F32)
    second = rest.astype(BF16)
    third = (rest - second.astype(F32)).astype(BF16)
    return first, second, third


def pack_kernel(
    state_in, cot_in, col_embed_in, row_embed_in, field, first, last, payload,
    state, cot, col_embed_t, row_embed, sem,
):
    small = [begin(col_embed_in, col_embed_t, sem.at[0]), begin(row_embed_in, row_embed, sem.at[1])]
    pieces = []
    for tile in (0, 2, 1):
        lanes = slice(tile * T, (tile + 1) * T)
        for half, origin, target in ((0, state_in, state), (1, cot_in, cot)):
            copy = begin(origin.at[:, :, lanes], target.at[:, :, lanes], sem.at[2 + 2 * tile + half])
            pieces.append((half, target, lanes, copy))
    for copy in small:
        copy.wait()
    wide = row_embed[...].astype(F32)
    edges = jnp.concatenate(
        [wide[0:R], wide[H - R : H], jnp.zeros((T - 2 * R, C), F32)], axis=0
    ).astype(BF16)
    extra = dot_nt(identity(C), edges).astype(BF16)
    for peer in range(N):
        payload[peer, :, 0:W] = col_embed_t[...]
        payload[peer, :, W:L] = extra
    for half, source, lanes, copy in pieces:
        copy.wait()
        field[:, half * C : (half + 1) * C, lanes] = jnp.swapaxes(source[:, :, lanes], 0, 1)
    lane = lane_iota(2 * C, T)
    for group in range(2):
        head = jnp.zeros((2 * C, T), BF16)
        tail = jnp.zeros((2 * C, T), BF16)
        for slot in range(16):
            h = group * 16 + slot
            here = (lane >= slot * R) & (lane < slot * R + R)
            left = field[h, :, 0:T]
            right = field[h, :, W - T : W]
            head = jnp.where(here, pltpu.roll(left, slot * R, 1) if slot else left, head)
            turn = (slot * R + R) % T
            tail = jnp.where(here, pltpu.roll(right, turn, 1) if turn else right, tail)
        first[:, group * T : (group + 1) * T] = head
        last[:, group * T : (group + 1) * T] = tail


def sides_kernel(from_right, from_left, field, side, top, bottom):
    lane = lane_iota(2 * C, T)
    zero = jnp.zeros((2 * C, T), BF16)
    for h in range(H):
        group, slot = divmod(h, 16)
        lanes = slice(group * T, (group + 1) * T)
        right = from_right[:, lanes]
        left = from_left[:, lanes]
        if slot:
            right = pltpu.roll(right, T - slot * R, 1)
        turn = (T - R - slot * R) % T
        if turn:
            left = pltpu.roll(left, turn, 1)
        both = jnp.where(lane < R, right, jnp.where(lane >= T - R, left, zero))
        side[h] = both
        if h < R:
            top[h, :, W:L] = both
        if h >= H - R:
            bottom[h - H + R, :, W:L] = both
    top[:, :, 0:W] = field[0:R]
    bottom[:, :, 0:W] = field[H - R : H]


def features_kernel(gathered, row_embed, col_proj_t, feat, payload):
    me = lax.axis_index("row")
    columns = jnp.dot(col_proj_t[...], gathered[...].reshape(N * C, L), preferred_element_type=F32)
    feat[...] = columns
    own = jnp.concatenate([row_embed[...].astype(F32), jnp.zeros((T - H, C), F32)], axis=0).astype(BF16)
    out = dot_nt(identity(C), own)
    above = gathered[lax.rem(me + N - 1, N), :, W:L].astype(F32)
    below = gathered[lax.rem(me + 1, N), :, W:L].astype(F32)
    high = columns.astype(BF16).astype(F32)
    low = columns - high
    lane = lane_iota(C, T)

    def put(out, start, source, origin):
        turn = (start - origin) % T
        moved = pltpu.roll(source, turn, 1) if turn else source
        return jnp.where((lane >= start) & (lane < start + R), moved, out)

    out = put(out, 32, above, 8)
    out = put(out, 40, below, 0)
    out = put(out, 48, high[:, 0:T], 0)
    out = put(out, 56, high[:, W - T : W], T - R)
    out = put(out, 64, low[:, 0:T], 0)
    out = put(out, 72, low[:, W - T : W], T - R)
    out = out.astype(BF16)
    for peer in range(N):
        payload[peer] = out


BAND = 3 * C
TAPS = 9 * C
SPAN = 6 * T


def band_kernel(conv_one, conv_two, one_out, one_t_out, two_out, two_t_out, one, one_t, two, two_t, sem):
    eye = identity(C)

    def fill(out, weights, transposed):
        if transposed:
            stacked = jnp.concatenate([weights[8 - tap].astype(F32) for tap in range(9)], axis=0).astype(BF16)
            block = dot_nt(eye, stacked)
        else:
            block = jnp.concatenate([weights[tap].astype(F32) for tap in range(9)], axis=1)
        block = jnp.concatenate([block, jnp.zeros((C, SPAN - TAPS), F32)], axis=1)
        for t in range(5):
            moved = pltpu.roll(block, t * BAND, 1) if t else block
            out[t * C : (t + 1) * C, :] = moved.astype(BF16)

    copies = []
    for k, (scratch, out, weights, transposed) in enumerate((
        (two_t, two_t_out, conv_two, True), (one, one_out, conv_one, False),
        (one_t, one_t_out, conv_one, True), (two, two_out, conv_two, False),
    )):
        fill(scratch, weights, transposed)
        copies.append(begin(scratch, out, sem.at[k]))
    for copy in copies:
        copy.wait()


def put(rows, i, value):
    rows[i, C : 2 * C] = value


def shift(rows, count):
    for i in range(count):
        value = rows[i, C : 2 * C]
        rows[i, 0:C] = pltpu.roll(value, 4, 1)
        rows[i, 2 * C : 3 * C] = pltpu.roll(value, L - 4, 1)


def conv_rows(band, rows, count):
    per = 5 if count == H + R else 4
    matrix = band[0 : C * per, 0 : BAND * (per + 2)]
    for residue in range(4):
        for group in range(2):
            start = residue + 4 * per * group
            stacked = jnp.concatenate([rows[start + 4 * s] for s in range(per + 2)], axis=0)
            product = jnp.dot(matrix, stacked, preferred_element_type=F32)
            for t in range(per):
                yield residue, per * group + t, product[t * C : (t + 1) * C]


def inside():
    row = lax.axis_index("row")
    col = lax.axis_index("col")
    left = jnp.where(col > 0, 1.0, 0.0)
    right = jnp.where(col < N - 1, 1.0, 0.0)
    lanes = jnp.where(lane_iota(C, T) < T // 2, right, left)
    return lanes, jnp.where(row > 0, 1.0, 0.0), jnp.where(row < N - 1, 1.0, 0.0)


def cot_kernel(field, side, above, below, band, out, rows, result, sem):
    lanes, up, down = inside()
    for i in range(H):
        last = (side[i, C : 2 * C, :].astype(F32) * lanes).astype(BF16)
        put(rows, R + i, jnp.concatenate([field[i, C : 2 * C, :], last], axis=1))
    wide = jnp.concatenate([jnp.ones((C, W), F32), lanes], axis=1)
    for i in range(R):
        put(rows, i, (above[i, C : 2 * C, :].astype(F32) * (wide * up)).astype(BF16))
        put(rows, R + H + i, (below[i, C : 2 * C, :].astype(F32) * (wide * down)).astype(BF16))
    shift(rows, H + 2 * R)
    copies = []
    for residue, place, value in conv_rows(band, rows, H + R):
        result[residue, place] = value.astype(BF16)
        if place == (H + R) // 4 - 1:
            copies.append(begin(result.at[residue], out.at[residue], sem.at[residue]))
    for copy in copies:
        copy.wait()


def main_kernel(
    field, side, above_in, below_in, d_active_in, col_feat, gathered, row_proj_t, one_in, one_t_in, two_in, bias, bias_two,
    pair_out, state_grad, col_part, row_part,
    rows, active, grads, above, below, d_active, one, one_t, two, pair_rows, grad_rows, pair_turned, grad_turned,
    sums, sem,
):
    edges = [begin(above_in, above, sem.at[0]), begin(below_in, below, sem.at[1])]
    band = begin(one_in, one, sem.at[2])
    slopes = [begin(d_active_in.at[q], d_active.at[q], sem.at[4 + q]) for q in range(4)]
    band_t = begin(one_t_in, one_t, sem.at[3])
    band_two = begin(two_in, two, sem.at[8])
    col = lax.axis_index("col")
    lane = lane_iota(C, T)
    lanes, up, down = inside()
    row_feat = jnp.dot(row_proj_t[...], gathered[...].reshape(N * C, T), preferred_element_type=F32)
    right = gathered[lax.rem(col + 1, N)].astype(F32)
    left = gathered[lax.rem(col + N - 1, N)].astype(F32)
    right = pltpu.roll(right, T - 48, 1) + pltpu.roll(right, T - 64, 1)
    left = pltpu.roll(left, T - R - 56, 1) + pltpu.roll(left, T - R - 72, 1)
    columns = jnp.concatenate([col_feat[:, 0:W], jnp.where(lane < T // 2, right, left)], axis=1)
    wide = jnp.concatenate([jnp.ones((C, W), F32), lanes], axis=1)

    def assemble(value, place):
        return value.astype(F32) + (columns + row_feat[:, place : place + 1])

    for i in range(H):
        value = assemble(jnp.concatenate([field[i, 0:C, :], side[i, 0:C, :]], axis=1), i)
        value = jnp.concatenate([value[:, 0:W], value[:, W:L] * lanes], axis=1)
        put(rows, R + i, value.astype(BF16))
    for copy in edges:
        copy.wait()
    for i in range(R):
        put(rows, i, (assemble(above[i, 0:C, :], H + i) * (wide * up)).astype(BF16))
        place = R + H + i
        put(rows, place, (assemble(below[i, 0:C, :], place) * (wide * down)).astype(BF16))
    shift(rows, H + 2 * R)
    copies = []

    def finish(source, target, out, first):
        for tile in range(TILES):
            part = slice(tile * T, (tile + 1) * T)
            target[:, :, part] = jnp.swapaxes(source[:, :, part], 0, 1)
            copies.append(begin(target.at[:, :, part], out.at[:, :, part], sem.at[first + tile]))


    first_bias = bias[...]
    band.wait()
    for residue, place, value in conv_rows(one, rows, H + R):
        if place == 0:
            slopes[residue].wait()
        i = residue + 4 * place
        hidden = value + first_bias
        sigma = 0.5 + 0.5 * jnp.tanh(0.5 * hidden)
        slope = sigma * (1.0 + hidden * (1.0 - sigma))

        def clip(value):
            value = jnp.concatenate([value[:, 0:W], value[:, W:L] * lanes], axis=1)
            if i < R // 2:
                value = value * up
            if i >= H + R // 2:
                value = value * down
            return value.astype(BF16)

        put(active, i, clip(hidden * sigma))
        put(grads, i, clip(d_active[residue, place].astype(F32) * slope))

    shift(grads, H + R)
    band_t.wait()
    col_sum = jnp.zeros((C, W), F32)
    for residue, place, value in conv_rows(one_t, grads, H):
        i = residue + 4 * place
        d_pair = field[i, C : 2 * C, :].astype(F32) + value[:, 0:W]
        grad_rows[i] = d_pair.astype(BF16)
        col_sum = col_sum + d_pair
        sums[i * C : (i + 1) * C, :] = d_pair[:, 0:T] + d_pair[:, T : 2 * T] + d_pair[:, 2 * T : W]
    finish(grad_rows, grad_turned, state_grad, 9)
    col_out = col_sum.astype(BF16)
    for peer in range(N):
        col_part[peer] = col_out
    partial = sums[...]
    high = partial.astype(BF16)
    low = (partial - high.astype(F32)).astype(BF16)
    ones = jnp.ones((2 * T, T), BF16)
    totals = jnp.dot(jnp.concatenate([high, low], axis=1), ones, preferred_element_type=F32)
    row_sum = jnp.zeros((C, T), F32)
    for i in range(H):
        row_sum = jnp.where(lane == i, totals[i * C : (i + 1) * C], row_sum)
    row_part[...] = row_sum

    shift(active, H + R)
    band_two.wait()
    second_bias = bias_two[...]
    for residue, place, value in conv_rows(two, active, H):
        i = residue + 4 * place
        pair = rows[R + i, C : 2 * C, 0:W].astype(F32)
        pair_rows[i] = (pair + value[:, 0:W] + second_bias).astype(BF16)
    finish(pair_rows, pair_turned, pair_out, 12)
    for copy in copies:
        copy.wait()


def proj_slice(proj_t, axis):
    turn = lax.rem(L - lax.axis_index(axis) * C, L)
    return pltpu.roll(proj_t[...].astype(F32), turn, 1)[:, 0:T].astype(BF16)[:, 0:C]


def grads_kernel(row_total, col_gathered, row_proj_t, col_proj_t, grad_row, grad_col):
    weights = proj_slice(row_proj_t, "col")
    grad_row[...] = sum(dot_tn(part, weights) for part in split(row_total[...]))[0:H, :]
    total = jnp.sum(col_gathered[...].astype(F32), axis=0)
    weights = proj_slice(col_proj_t, "row")
    grad_col[...] = sum(dot_tn(weights, part) for part in split(total))


def everyone(blocks, axis):
    return lax.all_to_all(blocks, axis, 0, 0, tiled=True)


def on_device(
    pair_state, row_embed, col_embed, row_proj, col_proj, conv_one, conv_two, bias_one, bias_two, cotangent
):
    forward = [(i, (i + 1) % N) for i in range(N)]
    backward = [(j, i) for i, j in forward]
    field, first, last, payload = call(
        pack_kernel, "pack",
        (struct(H, 2 * C, W), struct(2 * C, 2 * T), struct(2 * C, 2 * T), struct(N, C, L)),
        (pair_state, cotangent, col_embed.T, row_embed), 10**6, 4 * 10**6,
        [
            pltpu.VMEM((C, H, W), BF16), pltpu.VMEM((C, H, W), BF16), pltpu.VMEM((C, W), BF16),
            pltpu.VMEM((H, C), BF16), pltpu.SemaphoreType.DMA((8,)),
        ],
        [HBM] * 4,
    )
    from_left = lax.ppermute(last, "col", forward)
    from_right = lax.ppermute(first, "col", backward)
    band = struct(C * 5, SPAN)
    one, one_t, two, two_t = call(
        band_kernel, "band", (band, band, band, band), (conv_one, conv_two), 10**6, 10**6,
        places=(HBM,) * 4,
        scratch=[pltpu.VMEM(band.shape, BF16)] * 4 + [pltpu.SemaphoreType.DMA((4,))],
    )
    from_left, from_right, one = lax.optimization_barrier((from_left, from_right, one))
    gathered = everyone(payload, "row")
    side, top, bottom = call(
        sides_kernel, "sides", (struct(H, 2 * C, T), struct(R, 2 * C, L), struct(R, 2 * C, L)),
        (from_right, from_left, field), 10**6, 2 * 10**6,
    )
    above = lax.ppermute(bottom, "row", forward)
    below = lax.ppermute(top, "row", backward)
    col_feat, payload = call(
        features_kernel, "features", (struct(C, L, dtype=F32), struct(N, C, T)),
        (gathered, row_embed, col_proj.T), 2 * C * L * L, 10**6,
    )
    gathered = everyone(payload, "col")
    spread = (4, (H + R) // 4, C, L)
    d_active = call(
        cot_kernel, "cot_conv", struct(*spread),
        (field, side, above, below, two_t), 3 * 10**9, 5 * 10**6,
        [pltpu.VMEM((H + 2 * R, BAND, L), BF16), pltpu.VMEM(spread, BF16), pltpu.SemaphoreType.DMA((4,))],
        places=HBM,
    )
    pair_out, state_grad, col_part, row_part = call(
        main_kernel, "main_step",
        (struct(C, H, W), struct(C, H, W), struct(N, C, W), struct(C, T, dtype=F32)),
        (
            field, side, above, below, d_active, col_feat, gathered, row_proj.T, one, one_t, two,
            bias_one[:, None], bias_two[:, None],
        ),
        6 * 10**9, 10**7,
        [
            pltpu.VMEM((H + 2 * R, BAND, L), BF16), pltpu.VMEM((H + R, BAND, L), BF16),
            pltpu.VMEM((H + R, BAND, L), BF16), pltpu.VMEM((R, 2 * C, L), BF16), pltpu.VMEM((R, 2 * C, L), BF16),
            pltpu.VMEM(spread, BF16), pltpu.VMEM(band.shape, BF16), pltpu.VMEM(band.shape, BF16),
            pltpu.VMEM(band.shape, BF16), pltpu.VMEM((H, C, W), BF16), pltpu.VMEM((H, C, W), BF16),
            pltpu.VMEM((C, H, W), BF16), pltpu.VMEM((C, H, W), BF16), pltpu.VMEM((H * C, T), F32),
            pltpu.SemaphoreType.DMA((15,)),
        ],
        [VMEM, VMEM, ANY, ANY, HBM, VMEM, VMEM, VMEM, HBM, HBM, HBM, VMEM, VMEM],
        (HBM, HBM, VMEM, VMEM),
    )
    col_all = everyone(col_part, "row")
    for step in (4, 1):
        moved = [
            lax.ppermute(row_part, "col", [(i, i ^ (step * k)) for i in range(N)]) for k in (1, 2, 3)
        ]
        row_part = (row_part + moved[0]) + (moved[1] + moved[2])
    grad_row, grad_col = call(
        grads_kernel, "grads", (struct(H, C, dtype=F32), struct(C, W, dtype=F32)),
        (row_part, col_all, row_proj.T, col_proj.T), 10**6, 10**6,
    )
    return pair_out, state_grad, grad_row, grad_col.T


def solution(mesh):
    placed = (
        P(None, "row", "col"),
        P("row", "col"),
        P("col", "row"),
        P(),
        P(),
        P(),
        P(),
        P(),
        P(),
        P(None, "row", "col"),
    )
    return jax.shard_map(
        on_device,
        mesh=mesh,
        in_specs=placed,
        out_specs=(P(None, "row", "col"), P(None, "row", "col"), P("row", "col"), P("col", "row")),
        check_vma=False,
    )
```

```python
import jax
import jax.numpy as jnp
from jax import lax
from jax.experimental import pallas as pl
from jax.experimental.pallas import tpu as pltpu
from jax.sharding import PartitionSpec as P

F32 = jnp.float32
BF16 = jnp.bfloat16
C = 32
H = 32
W = 384
L = 512
R = 8
T = 128
N = 16
TILES = W // T
VMEM_LIMIT = 30 * 1024 * 1024


def lane_iota(rows, lanes):
    return lax.broadcasted_iota(jnp.int32, (rows, lanes), 1)


def struct(*shape, dtype=BF16):
    return jax.ShapeDtypeStruct(shape, dtype)


VMEM = pl.BlockSpec(memory_space=pltpu.VMEM)
HBM = pl.BlockSpec(memory_space=pltpu.HBM)
ANY = pl.BlockSpec(memory_space=pl.ANY)


def in_hbm(outs, places):
    if not places:
        return outs
    if not isinstance(outs, tuple):
        return pltpu.HBM(outs.shape, outs.dtype)
    return tuple(pltpu.HBM(o.shape, o.dtype) if p is HBM else o for o, p in zip(outs, places))


def call(body, name, outs, args, flops, nbytes, scratch=(), ins=None, places=None):
    several = isinstance(outs, tuple)
    if ins:
        args = [
            pltpu.with_memory_space_constraint(arg, pltpu.HBM) if spec is HBM else arg
            for arg, spec in zip(args, ins)
        ]
    return pl.pallas_call(
        body,
        out_shape=in_hbm(outs, places),
        in_specs=ins or [VMEM] * len(args),
        out_specs=places or ((VMEM,) * len(outs) if several else VMEM),
        scratch_shapes=list(scratch),
        compiler_params=pltpu.CompilerParams(vmem_limit_bytes=VMEM_LIMIT),
        cost_estimate=pl.CostEstimate(flops=flops, bytes_accessed=nbytes, transcendentals=0),
        name=name,
    )(*args)


def begin(source, target, sem):
    copy = pltpu.make_async_copy(source, target, sem)
    copy.start()
    return copy


def dot_nt(a, b):
    return lax.dot_general(a, b, (((1,), (1,)), ((), ())), preferred_element_type=F32)


def identity(size):
    rows = lax.broadcasted_iota(jnp.int32, (size, size), 0)
    return (rows == lane_iota(size, size)).astype(BF16)


def dot_tn(a, b):
    return lax.dot_general(a, b, (((0,), (0,)), ((), ())), preferred_element_type=F32)


def split(value):
    first = value.astype(BF16)
    rest = value - first.astype(F32)
    second = rest.astype(BF16)
    third = (rest - second.astype(F32)).astype(BF16)
    return first, second, third


def pack_kernel(
    state_in, cot_in, col_embed_in, row_embed_in, field, first, last, payload,
    state, cot, col_embed_t, row_embed, sem,
):
    small = [begin(col_embed_in, col_embed_t, sem.at[0]), begin(row_embed_in, row_embed, sem.at[1])]
    pieces = []
    for tile in (0, 2, 1):
        lanes = slice(tile * T, (tile + 1) * T)
        for half, origin, target in ((0, state_in, state), (1, cot_in, cot)):
            copy = begin(origin.at[:, :, lanes], target.at[:, :, lanes], sem.at[2 + 2 * tile + half])
            pieces.append((half, target, lanes, copy))
    for copy in small:
        copy.wait()
    wide = row_embed[...].astype(F32)
    edges = jnp.concatenate(
        [wide[0:R], wide[H - R : H], jnp.zeros((T - 2 * R, C), F32)], axis=0
    ).astype(BF16)
    extra = dot_nt(identity(C), edges).astype(BF16)
    for peer in range(N):
        payload[peer, :, 0:W] = col_embed_t[...]
        payload[peer, :, W:L] = extra
    for half, source, lanes, copy in pieces:
        copy.wait()
        field[:, half * C : (half + 1) * C, lanes] = jnp.swapaxes(source[:, :, lanes], 0, 1)
    lane = lane_iota(2 * C, T)
    for group in range(2):
        head = jnp.zeros((2 * C, T), BF16)
        tail = jnp.zeros((2 * C, T), BF16)
        for slot in range(16):
            h = group * 16 + slot
            here = (lane >= slot * R) & (lane < slot * R + R)
            left = field[h, :, 0:T]
            right = field[h, :, W - T : W]
            head = jnp.where(here, pltpu.roll(left, slot * R, 1) if slot else left, head)
            turn = (slot * R + R) % T
            tail = jnp.where(here, pltpu.roll(right, turn, 1) if turn else right, tail)
        first[:, group * T : (group + 1) * T] = head
        last[:, group * T : (group + 1) * T] = tail


def sides_kernel(from_right, from_left, field, side, top, bottom, ends, sem):
    copies = [
        begin(field.at[0:R], top.at[:, :, 0:W], sem.at[0]),
        begin(field.at[H - R : H], bottom.at[:, :, 0:W], sem.at[1]),
    ]
    lane = lane_iota(2 * C, T)
    zero = jnp.zeros((2 * C, T), BF16)
    for h in [*range(R), *range(H - R, H), *range(R, H - R)]:
        group, slot = divmod(h, 16)
        lanes = slice(group * T, (group + 1) * T)
        right = from_right[:, lanes]
        left = from_left[:, lanes]
        if slot:
            right = pltpu.roll(right, T - slot * R, 1)
        turn = (T - R - slot * R) % T
        if turn:
            left = pltpu.roll(left, turn, 1)
        both = jnp.where(lane < R, right, jnp.where(lane >= T - R, left, zero))
        side[h] = both
        if h < R:
            ends[0, h] = both
        if h >= H - R:
            ends[1, h - H + R] = both
        if h == R - 1:
            copies.append(begin(ends.at[0], top.at[:, :, W:L], sem.at[2]))
        if h == H - 1:
            copies.append(begin(ends.at[1], bottom.at[:, :, W:L], sem.at[3]))
    for copy in copies:
        copy.wait()


def features_kernel(gathered, row_embed, col_proj_t, feat, payload):
    me = lax.axis_index("row")
    columns = jnp.dot(col_proj_t[...], gathered[...].reshape(N * C, L), preferred_element_type=F32)
    feat[...] = columns
    own = jnp.concatenate([row_embed[...].astype(F32), jnp.zeros((T - H, C), F32)], axis=0).astype(BF16)
    out = dot_nt(identity(C), own)
    above = gathered[lax.rem(me + N - 1, N), :, W:L].astype(F32)
    below = gathered[lax.rem(me + 1, N), :, W:L].astype(F32)
    high = columns.astype(BF16).astype(F32)
    low = columns - high
    lane = lane_iota(C, T)

    def put(out, start, source, origin):
        turn = (start - origin) % T
        moved = pltpu.roll(source, turn, 1) if turn else source
        return jnp.where((lane >= start) & (lane < start + R), moved, out)

    out = put(out, 32, above, 8)
    out = put(out, 40, below, 0)
    out = put(out, 48, high[:, 0:T], 0)
    out = put(out, 56, high[:, W - T : W], T - R)
    out = put(out, 64, low[:, 0:T], 0)
    out = put(out, 72, low[:, W - T : W], T - R)
    out = out.astype(BF16)
    for peer in range(N):
        payload[peer] = out


BAND = 3 * C
TAPS = 9 * C
SPAN = 6 * T


def band_kernel(conv_one, conv_two, one_out, one_t_out, two_out, two_t_out, one, one_t, two, two_t, sem):
    eye = identity(C)

    def fill(out, weights, transposed):
        if transposed:
            stacked = jnp.concatenate([weights[8 - tap].astype(F32) for tap in range(9)], axis=0).astype(BF16)
            block = dot_nt(eye, stacked)
        else:
            block = jnp.concatenate([weights[tap].astype(F32) for tap in range(9)], axis=1)
        block = jnp.concatenate([block, jnp.zeros((C, SPAN - TAPS), F32)], axis=1)
        for t in range(5):
            moved = pltpu.roll(block, t * BAND, 1) if t else block
            out[t * C : (t + 1) * C, :] = moved.astype(BF16)

    copies = []
    for k, (scratch, out, weights, transposed) in enumerate((
        (two_t, two_t_out, conv_two, True), (one, one_out, conv_one, False),
        (one_t, one_t_out, conv_one, True), (two, two_out, conv_two, False),
    )):
        fill(scratch, weights, transposed)
        copies.append(begin(scratch, out, sem.at[k]))
    for copy in copies:
        copy.wait()


def put(rows, i, value):
    rows[i, C : 2 * C] = value


def shift(rows, count):
    for i in range(count):
        value = rows[i, C : 2 * C]
        rows[i, 0:C] = pltpu.roll(value, 4, 1)
        rows[i, 2 * C : 3 * C] = pltpu.roll(value, L - 4, 1)


def conv_rows(band, rows, count):
    per = 5 if count == H + R else 4
    matrix = band[0 : C * per, 0 : BAND * (per + 2)]
    for residue in range(4):
        for group in range(2):
            start = residue + 4 * per * group
            stacked = jnp.concatenate([rows[start + 4 * s] for s in range(per + 2)], axis=0)
            product = jnp.dot(matrix, stacked, preferred_element_type=F32)
            for t in range(per):
                yield residue, per * group + t, product[t * C : (t + 1) * C]


def inside():
    row = lax.axis_index("row")
    col = lax.axis_index("col")
    left = jnp.where(col > 0, 1.0, 0.0)
    right = jnp.where(col < N - 1, 1.0, 0.0)
    lanes = jnp.where(lane_iota(C, T) < T // 2, right, left)
    return lanes, jnp.where(row > 0, 1.0, 0.0), jnp.where(row < N - 1, 1.0, 0.0)


def cot_kernel(field, side, above, below, band, out, rows, result, sem):
    lanes, up, down = inside()
    for i in range(H):
        last = (side[i, C : 2 * C, :].astype(F32) * lanes).astype(BF16)
        put(rows, R + i, jnp.concatenate([field[i, C : 2 * C, :], last], axis=1))
    wide = jnp.concatenate([jnp.ones((C, W), F32), lanes], axis=1)
    for i in range(R):
        put(rows, i, (above[i, C : 2 * C, :].astype(F32) * (wide * up)).astype(BF16))
        put(rows, R + H + i, (below[i, C : 2 * C, :].astype(F32) * (wide * down)).astype(BF16))
    shift(rows, H + 2 * R)
    copies = []
    for residue, place, value in conv_rows(band, rows, H + R):
        result[residue, place] = value.astype(BF16)
        if place == (H + R) // 4 - 1:
            copies.append(begin(result.at[residue], out.at[residue], sem.at[residue]))
    for copy in copies:
        copy.wait()


def main_kernel(
    field, side, above_in, below_in, d_active_in, col_feat, gathered, row_proj_t, one_in, one_t_in, two_in, bias, bias_two,
    pair_out, state_grad, col_part, row_part,
    rows, active, grads, above, below, d_active, one, one_t, two, pair_rows, grad_rows, pair_turned, grad_turned,
    sums, sem,
):
    edges = [begin(above_in, above, sem.at[0]), begin(below_in, below, sem.at[1])]
    band = begin(one_in, one, sem.at[2])
    slopes = [begin(d_active_in.at[q], d_active.at[q], sem.at[4 + q]) for q in range(4)]
    band_t = begin(one_t_in, one_t, sem.at[3])
    band_two = begin(two_in, two, sem.at[8])
    col = lax.axis_index("col")
    lane = lane_iota(C, T)
    lanes, up, down = inside()
    row_feat = jnp.dot(row_proj_t[...], gathered[...].reshape(N * C, T), preferred_element_type=F32)
    right = gathered[lax.rem(col + 1, N)].astype(F32)
    left = gathered[lax.rem(col + N - 1, N)].astype(F32)
    right = pltpu.roll(right, T - 48, 1) + pltpu.roll(right, T - 64, 1)
    left = pltpu.roll(left, T - R - 56, 1) + pltpu.roll(left, T - R - 72, 1)
    columns = jnp.concatenate([col_feat[:, 0:W], jnp.where(lane < T // 2, right, left)], axis=1)
    wide = jnp.concatenate([jnp.ones((C, W), F32), lanes], axis=1)

    def assemble(value, place):
        return value.astype(F32) + (columns + row_feat[:, place : place + 1])

    for i in range(H):
        value = assemble(jnp.concatenate([field[i, 0:C, :], side[i, 0:C, :]], axis=1), i)
        value = jnp.concatenate([value[:, 0:W], value[:, W:L] * lanes], axis=1)
        put(rows, R + i, value.astype(BF16))
    for copy in edges:
        copy.wait()
    for i in range(R):
        put(rows, i, (assemble(above[i, 0:C, :], H + i) * (wide * up)).astype(BF16))
        place = R + H + i
        put(rows, place, (assemble(below[i, 0:C, :], place) * (wide * down)).astype(BF16))
    shift(rows, H + 2 * R)
    copies = []

    def finish(source, target, out, first):
        for tile in range(TILES):
            part = slice(tile * T, (tile + 1) * T)
            target[:, :, part] = jnp.swapaxes(source[:, :, part], 0, 1)
            copies.append(begin(target.at[:, :, part], out.at[:, :, part], sem.at[first + tile]))


    first_bias = bias[...]
    band.wait()
    for residue, place, value in conv_rows(one, rows, H + R):
        if place == 0:
            slopes[residue].wait()
        i = residue + 4 * place
        hidden = value + first_bias
        sigma = 0.5 + 0.5 * jnp.tanh(0.5 * hidden)
        slope = sigma * (1.0 + hidden * (1.0 - sigma))

        def clip(value):
            value = jnp.concatenate([value[:, 0:W], value[:, W:L] * lanes], axis=1)
            if i < R // 2:
                value = value * up
            if i >= H + R // 2:
                value = value * down
            return value.astype(BF16)

        put(active, i, clip(hidden * sigma))
        put(grads, i, clip(d_active[residue, place].astype(F32) * slope))

    shift(grads, H + R)
    band_t.wait()
    col_sum = jnp.zeros((C, W), F32)
    for residue, place, value in conv_rows(one_t, grads, H):
        i = residue + 4 * place
        d_pair = field[i, C : 2 * C, :].astype(F32) + value[:, 0:W]
        grad_rows[i] = d_pair.astype(BF16)
        col_sum = col_sum + d_pair
        sums[i * C : (i + 1) * C, :] = d_pair[:, 0:T] + d_pair[:, T : 2 * T] + d_pair[:, 2 * T : W]
    finish(grad_rows, grad_turned, state_grad, 9)
    col_out = col_sum.astype(BF16)
    for peer in range(N):
        col_part[peer] = col_out
    partial = sums[...]
    high = partial.astype(BF16)
    low = (partial - high.astype(F32)).astype(BF16)
    ones = jnp.ones((2 * T, T), BF16)
    totals = jnp.dot(jnp.concatenate([high, low], axis=1), ones, preferred_element_type=F32)
    row_sum = jnp.zeros((C, T), F32)
    for i in range(H):
        row_sum = jnp.where(lane == i, totals[i * C : (i + 1) * C], row_sum)
    row_part[...] = row_sum

    shift(active, H + R)
    band_two.wait()
    second_bias = bias_two[...]
    for residue, place, value in conv_rows(two, active, H):
        i = residue + 4 * place
        pair = rows[R + i, C : 2 * C, 0:W].astype(F32)
        pair_rows[i] = (pair + value[:, 0:W] + second_bias).astype(BF16)
    finish(pair_rows, pair_turned, pair_out, 12)
    for copy in copies:
        copy.wait()


def add_kernel(first, second, third, fourth, out):
    out[...] = (first[...] + second[...]) + (third[...] + fourth[...])


def proj_slice(proj_t, axis):
    turn = lax.rem(L - lax.axis_index(axis) * C, L)
    return pltpu.roll(proj_t[...].astype(F32), turn, 1)[:, 0:T].astype(BF16)[:, 0:C]


def grads_kernel(row_total, col_gathered, row_proj_t, col_proj_t, grad_row, grad_col):
    weights = proj_slice(row_proj_t, "col")
    grad_row[...] = sum(dot_tn(part, weights) for part in split(row_total[...]))[0:H, :]
    total = jnp.sum(col_gathered[...].astype(F32), axis=0)
    weights = proj_slice(col_proj_t, "row")
    grad_col[...] = sum(dot_tn(weights, part) for part in split(total))


def everyone(blocks, axis):
    return lax.all_to_all(blocks, axis, 0, 0, tiled=True)


def on_device(
    pair_state, row_embed, col_embed, row_proj, col_proj, conv_one, conv_two, bias_one, bias_two, cotangent
):
    forward = [(i, (i + 1) % N) for i in range(N)]
    backward = [(j, i) for i, j in forward]
    field, first, last, payload = call(
        pack_kernel, "pack",
        (struct(H, 2 * C, W), struct(2 * C, 2 * T), struct(2 * C, 2 * T), struct(N, C, L)),
        (pair_state, cotangent, col_embed.T, row_embed), 10**6, 4 * 10**6,
        [
            pltpu.VMEM((C, H, W), BF16), pltpu.VMEM((C, H, W), BF16), pltpu.VMEM((C, W), BF16),
            pltpu.VMEM((H, C), BF16), pltpu.SemaphoreType.DMA((8,)),
        ],
        [HBM] * 4,
    )
    from_left = lax.ppermute(last, "col", forward)
    from_right = lax.ppermute(first, "col", backward)
    band = struct(C * 5, SPAN)
    one, one_t, two, two_t = call(
        band_kernel, "band", (band, band, band, band), (conv_one, conv_two), 10**6, 10**6,
        places=(HBM,) * 4,
        scratch=[pltpu.VMEM(band.shape, BF16)] * 4 + [pltpu.SemaphoreType.DMA((4,))],
    )
    from_left, from_right, one = lax.optimization_barrier((from_left, from_right, one))
    gathered = everyone(payload, "row")
    side, top, bottom = call(
        sides_kernel, "sides", (struct(H, 2 * C, T), struct(R, 2 * C, L), struct(R, 2 * C, L)),
        (from_right, from_left, field), 10**6, 2 * 10**6,
        [pltpu.VMEM((2, R, 2 * C, T), BF16), pltpu.SemaphoreType.DMA((4,))], places=(VMEM, HBM, HBM),
    )
    above = lax.ppermute(bottom, "row", forward)
    below = lax.ppermute(top, "row", backward)
    col_feat, payload = call(
        features_kernel, "features", (struct(C, L, dtype=F32), struct(N, C, T)),
        (gathered, row_embed, col_proj.T), 2 * C * L * L, 10**6,
    )
    gathered = everyone(payload, "col")
    spread = (4, (H + R) // 4, C, L)
    d_active = call(
        cot_kernel, "cot_conv", struct(*spread),
        (field, side, above, below, two_t), 3 * 10**9, 5 * 10**6,
        [pltpu.VMEM((H + 2 * R, BAND, L), BF16), pltpu.VMEM(spread, BF16), pltpu.SemaphoreType.DMA((4,))],
        places=HBM,
    )
    pair_out, state_grad, col_part, row_part = call(
        main_kernel, "main_step",
        (struct(C, H, W), struct(C, H, W), struct(N, C, W), struct(C, T, dtype=F32)),
        (
            field, side, above, below, d_active, col_feat, gathered, row_proj.T, one, one_t, two,
            bias_one[:, None], bias_two[:, None],
        ),
        6 * 10**9, 10**7,
        [
            pltpu.VMEM((H + 2 * R, BAND, L), BF16), pltpu.VMEM((H + R, BAND, L), BF16),
            pltpu.VMEM((H + R, BAND, L), BF16), pltpu.VMEM((R, 2 * C, L), BF16), pltpu.VMEM((R, 2 * C, L), BF16),
            pltpu.VMEM(spread, BF16), pltpu.VMEM(band.shape, BF16), pltpu.VMEM(band.shape, BF16),
            pltpu.VMEM(band.shape, BF16), pltpu.VMEM((H, C, W), BF16), pltpu.VMEM((H, C, W), BF16),
            pltpu.VMEM((C, H, W), BF16), pltpu.VMEM((C, H, W), BF16), pltpu.VMEM((H * C, T), F32),
            pltpu.SemaphoreType.DMA((15,)),
        ],
        [VMEM, VMEM, ANY, ANY, HBM, VMEM, VMEM, VMEM, HBM, HBM, HBM, VMEM, VMEM],
        (HBM, HBM, VMEM, VMEM),
    )
    col_all = everyone(col_part, "row")
    for step in (4, 1):
        moved = [
            lax.ppermute(row_part, "col", [(i, i ^ (step * k)) for i in range(N)]) for k in (1, 2, 3)
        ]
        if step == 4:
            row_part = call(add_kernel, "add", struct(C, T, dtype=F32), (row_part, *moved), 10**10, 10**5)
        else:
            row_part = (row_part + moved[0]) + (moved[1] + moved[2])
    grad_row, grad_col = call(
        grads_kernel, "grads", (struct(H, C, dtype=F32), struct(C, W, dtype=F32)),
        (row_part, col_all, row_proj.T, col_proj.T), 10**6, 10**6,
    )
    return pair_out, state_grad, grad_row, grad_col.T


def solution(mesh):
    placed = (
        P(None, "row", "col"),
        P("row", "col"),
        P("col", "row"),
        P(),
        P(),
        P(),
        P(),
        P(),
        P(),
        P(None, "row", "col"),
    )
    return jax.shard_map(
        on_device,
        mesh=mesh,
        in_specs=placed,
        out_specs=(P(None, "row", "col"), P(None, "row", "col"), P("row", "col"), P("col", "row")),
        check_vma=False,
    )
```
